32 devices in a mesh: ctx: 8 (over y, x, core), head: 4 (over z).
Axes of the slice: x: 2, y: 2, z: 4, core: 2. Of those that a mesh axis runs over, the one named last changes fastest.
Arguments:
- queries: bfloat16 [4096, 2048], P('ctx', 'head'), may hold values from -6 to 6
- keys: bfloat16 [4096, 2048], P('ctx', 'head'), may hold values from -0.59765625 to 0.59765625
- values: bfloat16 [4096, 2048], P('ctx', 'head'), may hold values from -6 to 6
- log_decay: float32 [4096, 16], P('ctx', 'head'), may hold values from -0.76 to 0, as said below
- gain: float32 [2048], P('head'), may hold values from 0.1 to 1.9
- upstream: bfloat16 [4096, 2048], P('ctx', 'head'), may hold values from -6 to 6
Outputs:
- grad_queries: bfloat16 [4096, 2048], P('ctx', 'head')
- grad_keys: bfloat16 [4096, 2048], P('ctx', 'head')
- grad_values: bfloat16 [4096, 2048], P('ctx', 'head')
The draws below stay inside these ranges and needn't reach their ends.
Inputs may be any that keep to these rules, and one draw needn't show every extreme that they name: `log_decay`: the logarithm of the decay that each head applies at each token.
All inputs are finite; a program needn't handle non-finite values.
Results may differ from the reference program's by a relative error of at most 0.0054.
Values sent between devices are 32-bit elements; how exact they have to be, the bound alone decides.
A program may use at most 64 MiB of HBM per device.

```python
import jax
import jax.numpy as jnp
from jax import lax

HEAD_DIM = 128
BLK = 512
HEADS = 16
WIDTH = 2048
SEQUENCE_LENGTH = 4096


def draw_log_decay(key, part):
    key = jax.random.fold_in(key, 11)
    complete_lookup_matrix = jax.random.split(key, 6)
    share = 0.5
    quick = jax.random.uniform(complete_lookup_matrix[0], (HEADS,)) < share
    slow_rate = jax.random.uniform(complete_lookup_matrix[1], (HEADS,), minval=0.02, maxval=0.12) / SEQUENCE_LENGTH
    quick_rate = jax.random.uniform(complete_lookup_matrix[2], (HEADS,), minval=1.0 / 50.0, maxval=1.0 / 30.0)
    baseline_decay_rate = jnp.where(quick, quick_rate, slow_rate)
    rough = jnp.exp(jax.random.uniform(complete_lookup_matrix[3], (SEQUENCE_LENGTH, HEADS), minval=-0.69, maxval=0.69))
    sequence_segments = jax.random.randint(complete_lookup_matrix[4], (2,), 0, SEQUENCE_LENGTH)
    masked_places = jnp.any(jnp.arange(SEQUENCE_LENGTH)[:, None] == sequence_segments[None, :], axis=1).astype(jnp.float32)
    depth = jax.random.uniform(complete_lookup_matrix[5], (HEADS,), minval=0.22, maxval=0.69)
    return (-(baseline_decay_rate[None, :] * rough + masked_places[:, None] * depth[None, :])).astype(jnp.float32)


def block_scale(rng, extent, pieces, low, largest):
    level = 1.0
    for position, shards_of in pieces:
        steps = jax.random.uniform(jax.random.fold_in(jax.random.fold_in(rng, 6), position), (shards_of,), jnp.float32, low / len(pieces), largest / len(pieces))
        level = level * jnp.repeat(jnp.exp(steps), extent[position] // shards_of).reshape((-1,) + (1,) * (len(extent) - 1 - position))
    return level


def normal_values(rng, dims, width, bound, pieces=(), dtype=jnp.bfloat16):
    drawn = width * jax.random.normal(rng, dims, jnp.float32)
    if pieces:
        drawn = drawn * block_scale(rng, dims, pieces, -0.22, 0.18)
    return jnp.clip(drawn, -bound, bound).astype(dtype)


def setup_inputs(seed: int = 0) -> dict:
    splits = jax.random.split(jax.random.key(seed), 7)
    queries = normal_values(splits[0], (SEQUENCE_LENGTH, WIDTH), 1.0, 6.0, ((0, 8), (1, 4)))
    keys = normal_values(splits[1], (SEQUENCE_LENGTH, WIDTH), 0.1, 0.59765625, ((0, 8), (1, 4)))
    values = normal_values(splits[2], (SEQUENCE_LENGTH, WIDTH), 1.0, 6.0, ((0, 8), (1, 4)))
    log_decay = draw_log_decay(jax.random.fold_in(splits[6], 71), 0)
    gain = jnp.clip(1.0 + 0.18 * jax.random.normal(splits[4], (WIDTH,), jnp.float32), 0.1, 1.9)
    upstream = normal_values(splits[5], (SEQUENCE_LENGTH, WIDTH), 1.0, 6.0, ((0, 8), (1, 4)))
    return {"queries": queries, "keys": keys, "values": values, "log_decay": log_decay, "gain": gain, "upstream": upstream}


HIGHEST = lax.Precision.HIGHEST
EPSILON = 1e-06

def widen(array):
    return lax.optimization_barrier(array.astype(jnp.bfloat16)).astype(jnp.float32)

def decay_matrix(cumulative):
    columns = cumulative.T
    spread = columns[:, :, None] - columns[:, None, :]
    positions = jnp.arange(cumulative.shape[0])
    causal = (positions[:, None] >= positions[None, :])[None]
    return jnp.where(causal, jnp.exp(jnp.where(causal, spread, 0.0)), 0.0)

def reference(queries, keys, values, log_decay, gain, upstream):
    block_count = SEQUENCE_LENGTH // BLK
    block_shape = (block_count, BLK, HEADS, HEAD_DIM)
    query_blocks = queries.reshape(block_shape)
    key_blocks = keys.reshape(block_shape)
    value_blocks = values.reshape(block_shape)
    cumulative = jnp.cumsum(log_decay.reshape(block_count, BLK, HEADS), axis=1)
    zero_state = jnp.zeros((HEADS, HEAD_DIM, HEAD_DIM), jnp.float32)

    def forward_block(carried_over_state, segment_members):
        query_block, key_block, value_block, cum_block = segment_members
        query_wide = query_block.astype(jnp.float32)
        key_wide = key_block.astype(jnp.float32)
        value_wide = value_block.astype(jnp.float32)
        total_block = cum_block[-1]
        decays = decay_matrix(cum_block)
        carried = jnp.einsum('the,hef->thf', query_wide, carried_over_state, precision=HIGHEST) * jnp.exp(cum_block)[:, :, None]
        scores = jnp.einsum('the,she->hts', query_wide, key_wide, precision=HIGHEST)
        mixing = widen(scores * decays)
        attended = carried + jnp.einsum('hts,shf->thf', mixing, value_wide, precision=HIGHEST)
        weighted_keys = widen(key_wide * jnp.exp(total_block[None, :] - cum_block)[:, :, None])
        new_state = jnp.exp(total_block)[:, None, None] * carried_over_state + jnp.einsum('she,shf->hef', weighted_keys, value_wide, precision=HIGHEST)
        return (new_state, (attended, carried_over_state))
    _, (attended_all, opening_indices) = lax.scan(forward_block, zero_state, (query_blocks, key_blocks, value_blocks, cumulative))
    attended = attended_all.reshape(SEQUENCE_LENGTH, WIDTH)
    scaled_grad = gain * upstream.astype(jnp.float32)
    square_sum = lax.optimization_barrier(jnp.sum(attended * attended, axis=1))
    mutual_accumulation = lax.optimization_barrier(jnp.sum(scaled_grad * attended, axis=1))
    inverse = lax.rsqrt(square_sum / WIDTH + EPSILON)
    grad_out = (inverse[:, None] * scaled_grad - attended * (inverse * inverse * inverse * mutual_accumulation / WIDTH)[:, None]).astype(jnp.bfloat16)
    grad_blocks = grad_out.reshape(block_shape)

    def backward_block(after_state, segment_members):
        query_block, key_block, value_block, grad_block, cum_block, start_block = segment_members
        query_wide = query_block.astype(jnp.float32)
        key_wide = key_block.astype(jnp.float32)
        value_wide = value_block.astype(jnp.float32)
        grad_wide = grad_block.astype(jnp.float32)
        total_block = cum_block[-1]
        decays = decay_matrix(cum_block)
        ending_block = jnp.exp(total_block[None, :] - cum_block)[:, :, None]
        mixing = widen(jnp.einsum('the,she->hts', query_wide, key_wide, precision=HIGHEST) * decays)
        grad_mixing = widen(jnp.einsum('thf,shf->hts', grad_wide, value_wide, precision=HIGHEST) * decays)
        grad_query = jnp.einsum('thf,hef->the', grad_wide, start_block, precision=HIGHEST) * jnp.exp(cum_block)[:, :, None]
        grad_query = grad_query + jnp.einsum('hts,she->the', grad_mixing, key_wide, precision=HIGHEST)
        grad_key = jnp.einsum('shf,hef->she', value_wide, after_state, precision=HIGHEST) * ending_block
        grad_key = grad_key + jnp.einsum('hts,the->she', grad_mixing, query_wide, precision=HIGHEST)
        grad_value = jnp.einsum('she,hef->shf', key_wide, after_state, precision=HIGHEST) * ending_block
        grad_value = grad_value + jnp.einsum('hts,thf->shf', mixing, grad_wide, precision=HIGHEST)
        weighted_queries = widen(query_wide * jnp.exp(cum_block)[:, :, None])
        before_state = jnp.exp(total_block)[:, None, None] * after_state + jnp.einsum('the,thf->hef', weighted_queries, grad_wide, precision=HIGHEST)
        return (before_state, (grad_query.astype(jnp.bfloat16), grad_key.astype(jnp.bfloat16), grad_value.astype(jnp.bfloat16)))
    _, (grad_q_all, grad_k_all, grad_v_all) = lax.scan(backward_block, zero_state, (query_blocks, key_blocks, value_blocks, grad_blocks, cumulative, opening_indices), reverse=True)
    return (grad_q_all.reshape(SEQUENCE_LENGTH, WIDTH), grad_k_all.reshape(SEQUENCE_LENGTH, WIDTH), grad_v_all.reshape(SEQUENCE_LENGTH, WIDTH))
```

```python
import functools

import jax
import jax.numpy as jnp
from jax import lax
from jax.experimental import pallas as pl
from jax.experimental.pallas import tpu as pltpu
from jax.sharding import PartitionSpec as P

DIM = 128
TILE = 256
EPSILON = 1e-06
MESH = pl.DeviceIdType.MESH
F32 = jnp.float32
BF16 = jnp.bfloat16


def dot(a, b, dims):
    return lax.dot_general(a, b, ((dims[:1], dims[1:]), ((), ())), preferred_element_type=F32)


def split(x):
    high = x.astype(BF16)
    return high, (x - high.astype(F32)).astype(BF16)


def kernel(
    ctx_n, head_n, width,
    q_hbm, k_hbm, v_hbm, ld_hbm, gain_hbm, up_hbm,
    dq_out, dk_out, dv_out,
    q, k, v, ld, gain, up,
    mix, dec, att, grad, wq, cum, cum_rows, dkp, dvp, dq, dk, dv,
    f_send, f_recv, f_tsend, f_trecv, f_pre,
    b_send, b_recv, b_tsend, b_trecv, b_pre,
    z_send, z_recv,
    in_sem, out_sem,
    fs_sem, fr_sem, fts_sem, ftr_sem, fps_sem, fpr_sem,
    bs_sem, br_sem, bts_sem, btr_sem, bps_sem, bpr_sem,
    zs_sem, zr_sem,
):
    tokens = q.shape[0]
    heads = q.shape[1] // DIM
    half = heads // 2
    bits = ctx_n.bit_length() - 1
    tiles = tokens // TILE
    me = lax.axis_index("ctx")
    zed = lax.axis_index("head")
    core = lax.rem(me, 2)
    own = core * half
    bit_values = [lax.rem(me // (2**b), 2) for b in range(bits)]
    partners = [me + (2**b) * (1 - 2 * bit_values[b]) for b in range(bits)]

    loads = []
    for i, (src, dst) in enumerate(
        ((ld_hbm, ld), (k_hbm, k), (v_hbm, v), (q_hbm, q), (gain_hbm, gain), (up_hbm, up))
    ):
        load = pltpu.make_async_copy(src, dst, in_sem.at[i])
        load.start()
        loads.append(load)
    load_ld, load_k, load_v, load_q, load_gain, load_up = loads

    barrier = pltpu.get_barrier_semaphore()
    for b in range(bits):
        pl.semaphore_signal(barrier, inc=1, device_id=(partners[b], zed), device_id_type=MESH)
    for d in range(1, head_n):
        pl.semaphore_signal(
            barrier, inc=1, device_id=(me, lax.rem(zed + d, head_n)), device_id_type=MESH
        )

    load_ld.wait()
    steps = jnp.pad(ld[...], ((0, 0), (0, DIM - heads)))
    row_id = lax.broadcasted_iota(jnp.int32, (tokens, tokens), 0)
    col_id = lax.broadcasted_iota(jnp.int32, (tokens, tokens), 1)
    lower = jnp.where(row_id >= col_id, 1.0, 0.0).astype(BF16)
    top, rest = split(steps)
    low = (steps - top.astype(F32) - rest.astype(F32)).astype(BF16)
    total_cum = dot(lower, top, (1, 0)) + (dot(lower, rest, (1, 0)) + dot(lower, low, (1, 0)))
    cum[...] = total_cum
    cum_rows[...] = total_cum.T[:8]

    def columns(h):
        return slice(h * DIM, (h + 1) * DIM)

    def cum_column(h):
        return cum[:, h : h + 1]

    def total(h):
        return cum[tokens - 1 : tokens, h : h + 1]

    def level_rows(h):
        return jnp.broadcast_to(total(h), (8, DIM))

    diagonal = lax.broadcasted_iota(jnp.int32, (TILE, TILE), 0) >= lax.broadcasted_iota(
        jnp.int32, (TILE, TILE), 1
    )

    def exchange(rev, send, recv, tsend, trecv, pre, ss, rs, tss, trs, pss, prs):
        pending = []
        state = {}

        def remote(src, dst, s_sem, r_sem, b):
            copy = pltpu.make_async_remote_copy(
                src_ref=src, dst_ref=dst, send_sem=s_sem, recv_sem=r_sem,
                device_id=(partners[b], zed), device_id_type=MESH,
            )
            copy.start()
            pending.append(copy)
            return copy

        def upper(b):
            return (1 - bit_values[b]) if rev else bit_values[b]

        first = []

        def post(h, value):
            send[h, :DIM] = value
            send[h, DIM:] = level_rows(h)
            first.append(remote(send.at[h], recv.at[h], ss.at[h], rs.at[h], 0))

        def pair():
            for copy in first:
                copy.wait_recv()
            is_upper = upper(0) == 1
            for i in range(half):
                o = own + i
                mine, other = send[o, :DIM], recv[o, :DIM]
                my_level, other_level = send[o, DIM : DIM + 1], recv[o, DIM : DIM + 1]
                value = mine * jnp.where(is_upper, 1.0, jnp.exp(other_level)) + other * jnp.where(
                    is_upper, jnp.exp(my_level), 1.0
                )
                state[i] = (value, my_level + other_level, None, None)
                publish(1, i)

        copies = {}

        def publish(b, i):
            value, level, _, _ = state[i]
            slot = (b - 1) * half + i
            tsend[slot, :DIM] = value
            tsend[slot, DIM:] = jnp.broadcast_to(level, (8, DIM))
            copies[b, i] = remote(tsend.at[slot], trecv.at[slot], tss.at[slot], trs.at[slot], b)

        def combine(b):
            is_upper = upper(b) == 1
            for i in range(half):
                copies[b, i].wait_recv()
                slot = (b - 1) * half + i
                _, level, _, before_level = state[i]
                value = tsend[slot, :DIM]
                other, other_level = trecv[slot, :DIM], trecv[slot, DIM : DIM + 1]
                if before_level is None:
                    before = jnp.where(is_upper, other, 0.0)
                    before_level = jnp.where(is_upper, other_level, 0.0)
                else:
                    before = pre[own + i] + jnp.where(is_upper, jnp.exp(before_level), 0.0) * other
                    before_level = before_level + jnp.where(is_upper, other_level, 0.0)
                pre[own + i] = before
                if b + 1 < bits:
                    value = value * jnp.where(is_upper, 1.0, jnp.exp(other_level)) + (
                        other * jnp.where(is_upper, jnp.exp(level), 1.0)
                    )
                    state[i] = (value, level + other_level, None, before_level)
                    publish(b + 1, i)
                else:
                    copies["pre", i] = remote(
                        pre.at[own + i], pre.at[own + i], pss.at[i], prs.at[i], 0
                    )

        def finish():
            for i in range(half):
                copies["pre", i].wait_recv()
            for copy in pending:
                copy.wait_send()

        def result(h):
            outside = pre[h]
            level = recv[h, DIM : DIM + 1]
            return jnp.where(upper(0) == 1, outside * jnp.exp(level) + recv[h, :DIM], outside)

        stages = [pair] + [functools.partial(combine, b) for b in range(1, bits)] + [finish]
        return post, stages, result

    post, stages, start_state = exchange(
        False, f_send, f_recv, f_tsend, f_trecv, f_pre,
        fs_sem, fr_sem, fts_sem, ftr_sem, fps_sem, fpr_sem,
    )

    load_k.wait()
    load_v.wait()
    entered = bits + head_n - 1
    for h in range(heads):
        ending = jnp.exp(total(h) - cum_column(h))
        weighted_keys = (k[:, columns(h)].astype(F32) * ending).astype(BF16)
        value = dot(weighted_keys, v[:, columns(h)], (0, 0))
        if h == 0:
            pl.semaphore_wait(barrier, entered)
        post(h, value)

    load_q.wait()

    def forward(h):
        for i in range(tiles):
            rows = slice(i * TILE, (i + 1) * TILE)
            total_rows = None
            for j in range(i + 1):
                sources = slice(j * TILE, (j + 1) * TILE)
                scores = dot(q[rows, columns(h)], k[sources, columns(h)], (1, 1))
                spread = cum[rows, h : h + 1] - cum_rows[h : h + 1, sources]
                if i == j:
                    spread = jnp.where(diagonal, spread, -1e30)
                decays = jnp.exp(spread)
                dec[h, rows, sources] = decays
                mixing = (scores * decays).astype(BF16)
                mix[h, rows, sources] = mixing
                part = dot(mixing, v[sources, columns(h)], (1, 0))
                total_rows = part if total_rows is None else total_rows + part
            att[rows, columns(h)] = total_rows

    def weigh_queries(h):
        wq[:, columns(h)] = (q[:, columns(h)].astype(F32) * jnp.exp(cum_column(h))).astype(BF16)

    def interleave(works, stages):
        for place in range(max(len(works), len(stages))):
            if place < len(works):
                works[place]()
            if place < len(stages):
                stages[place]()

    interleave([functools.partial(forward, h) for h in range(heads)], stages)

    load_gain.wait()
    load_up.wait()
    squares = None
    for h in range(heads):
        high, low = split(start_state(h))
        queries = q[:, columns(h)]
        carried = dot(
            jnp.concatenate([queries, queries], axis=1), jnp.concatenate([high, low], axis=0), (1, 0)
        )
        value = att[:, columns(h)] + jnp.exp(cum_column(h)) * carried
        att[:, columns(h)] = value
        scaled = gain[:, columns(h)] * up[:, columns(h)].astype(F32)
        square, cross = value * value, scaled * value
        squares = square if squares is None else squares + square
        crosses = cross if h == 0 else crosses + cross
    square_sum = jnp.sum(squares, axis=1, keepdims=True)
    cross_sum = jnp.sum(crosses, axis=1, keepdims=True)
    lane = lax.broadcasted_iota(jnp.int32, (tokens, DIM), 1)
    packed = jnp.where(lane == 0, square_sum, jnp.where(lane == 1, cross_sum, 0.0))
    z_send[...] = packed.T[:8]
    z_copies = []
    for d in range(1, head_n):
        copy = pltpu.make_async_remote_copy(
            src_ref=z_send, dst_ref=z_recv.at[d - 1],
            send_sem=zs_sem.at[d - 1], recv_sem=zr_sem.at[d - 1],
            device_id=(me, lax.rem(zed + d, head_n)), device_id_type=MESH,
        )
        copy.start()
        z_copies.append(copy)
    for h in range(heads):
        weigh_queries(h)
    sums = z_send[...]
    for d in range(1, head_n):
        z_copies[d - 1].wait_recv()
        sums = sums + z_recv[d - 1]
    full = jnp.concatenate([sums, jnp.zeros((DIM - 8, tokens), F32)], axis=0).T
    square_sum, cross_sum = full[:, 0:1], full[:, 1:2]
    inverse = lax.rsqrt(square_sum / width + EPSILON)
    factor = inverse * inverse * inverse * cross_sum / width

    post, stages, end_state = exchange(
        True, b_send, b_recv, b_tsend, b_trecv, b_pre,
        bs_sem, br_sem, bts_sem, btr_sem, bps_sem, bpr_sem,
    )
    for h in range(heads):
        scaled = gain[:, columns(h)] * up[:, columns(h)].astype(F32)
        value = (inverse * scaled - att[:, columns(h)] * factor).astype(BF16)
        grad[:, columns(h)] = value
        post(h, dot(wq[:, columns(h)], value, (0, 0)))
    for copy in z_copies:
        copy.wait_send()

    stores = []

    def store(i, h, src, dst):
        copy = pltpu.make_async_copy(
            src.at[:, columns(h)], dst.at[:, columns(h)], out_sem.at[i * heads + h]
        )
        copy.start()
        stores.append(copy)

    def backward(h):
        high, low = split(start_state(h))
        states = jnp.concatenate([high, low], axis=1)
        key_sums, value_sums = [None] * tiles, [None] * tiles
        for i in range(tiles):
            rows = slice(i * TILE, (i + 1) * TILE)
            grads = grad[rows, columns(h)]
            query_sum = jnp.exp(cum[rows, h : h + 1]) * dot(
                jnp.concatenate([grads, grads], axis=1), states, (1, 1)
            )
            for j in range(i + 1):
                sources = slice(j * TILE, (j + 1) * TILE)
                scores = dot(grads, v[sources, columns(h)], (1, 1))
                mixing = (scores * dec[h, rows, sources]).astype(BF16)
                query_sum = query_sum + dot(mixing, k[sources, columns(h)], (1, 0))
                key_part = dot(mixing, q[rows, columns(h)], (0, 0))
                value_part = dot(mix[h, rows, sources], grads, (0, 0))
                key_sums[j] = key_part if i == j else key_sums[j] + key_part
                value_sums[j] = value_part if i == j else value_sums[j] + value_part
            dq[rows, columns(h)] = query_sum.astype(BF16)
        store(0, h, dq, dq_out)
        for j in range(tiles):
            sources = slice(j * TILE, (j + 1) * TILE)
            dkp[sources, columns(h)] = key_sums[j]
            dvp[sources, columns(h)] = value_sums[j]

    interleave([functools.partial(backward, h) for h in range(heads)], stages)

    for h in range(heads):
        high, low = split(end_state(h))
        ending = jnp.exp(total(h) - cum_column(h))
        keys, values = k[:, columns(h)], v[:, columns(h)]
        key_carried = dot(
            jnp.concatenate([values, values], axis=1), jnp.concatenate([high, low], axis=1), (1, 1)
        )
        dk[:, columns(h)] = (ending * key_carried + dkp[:, columns(h)]).astype(BF16)
        store(1, h, dk, dk_out)
        value_carried = dot(
            jnp.concatenate([keys, keys], axis=1), jnp.concatenate([high, low], axis=0), (1, 0)
        )
        dv[:, columns(h)] = (ending * value_carried + dvp[:, columns(h)]).astype(BF16)
        store(2, h, dv, dv_out)
    for copy in stores:
        copy.wait()


def on_device(queries, keys, values, log_decay, gain, upstream):
    tokens, local = queries.shape
    heads = log_decay.shape[1]
    ctx_n, head_n = lax.axis_size("ctx"), lax.axis_size("head")
    steps = ctx_n.bit_length() - 2
    half = heads // 2
    wide = (tokens, local)
    message = (heads, DIM + 8, DIM)
    chip_message = (steps * half, DIM + 8, DIM)
    states = [
        pltpu.VMEM(message, F32),
        pltpu.VMEM(message, F32),
        pltpu.VMEM(chip_message, F32),
        pltpu.VMEM(chip_message, F32),
        pltpu.VMEM((heads, DIM, DIM), F32),
    ]
    dma = pltpu.SemaphoreType.DMA
    state_sems = [
        dma((heads,)), dma((heads,)), dma((steps * half,)), dma((steps * half,)),
        dma((half,)), dma((half,)),
    ]
    anywhere = pl.BlockSpec(memory_space=pl.ANY)
    out = jax.ShapeDtypeStruct(wide, BF16)
    return pl.pallas_call(
        functools.partial(kernel, ctx_n, head_n, local * head_n),
        out_shape=(out, out, out),
        in_specs=[anywhere] * 6,
        out_specs=(anywhere,) * 3,
        scratch_shapes=[
            pltpu.VMEM(wide, BF16),
            pltpu.VMEM(wide, BF16),
            pltpu.VMEM(wide, BF16),
            pltpu.VMEM(log_decay.shape, F32),
            pltpu.VMEM((1, local), F32),
            pltpu.VMEM(wide, BF16),
            pltpu.VMEM((heads, tokens, tokens), BF16),
            pltpu.VMEM((heads, tokens, tokens), F32),
            pltpu.VMEM(wide, F32),
            pltpu.VMEM(wide, BF16),
            pltpu.VMEM(wide, BF16),
            pltpu.VMEM((tokens, DIM), F32),
            pltpu.VMEM((8, tokens), F32),
            pltpu.VMEM(wide, F32),
            pltpu.VMEM(wide, F32),
            pltpu.VMEM(wide, BF16),
            pltpu.VMEM(wide, BF16),
            pltpu.VMEM(wide, BF16),
            *states,
            *states,
            pltpu.VMEM((8, tokens), F32),
            pltpu.VMEM((head_n - 1, 8, tokens), F32),
            dma((6,)),
            dma((3 * heads,)),
            *state_sems,
            *state_sems,
            dma((head_n - 1,)),
            dma((head_n - 1,)),
        ],
        compiler_params=pltpu.CompilerParams(
            collective_id=0, has_side_effects=True, vmem_limit_bytes=48 * 2**20
        ),
        cost_estimate=pl.CostEstimate(
            flops=16 * heads * tokens * tokens * DIM,
            bytes_accessed=14 * tokens * local,
            transcendentals=heads * tokens * tokens,
        ),
    )(queries, keys, values, log_decay, gain.reshape(1, -1), upstream)


def solution(mesh):
    wide = P("ctx", "head")
    return jax.shard_map(
        on_device,
        mesh=mesh,
        in_specs=(wide, wide, wide, wide, P("head"), wide),
        out_specs=(wide, wide, wide),
        check_vma=False,
    )
```

```python
import functools

import jax
import jax.numpy as jnp
from jax import lax
from jax.experimental import pallas as pl
from jax.experimental.pallas import tpu as pltpu
from jax.sharding import PartitionSpec as P

DIM = 128
TILE = 256
EPSILON = 1e-06
MESH = pl.DeviceIdType.MESH
F32 = jnp.float32
BF16 = jnp.bfloat16


def dot(a, b, dims):
    return lax.dot_general(a, b, ((dims[:1], dims[1:]), ((), ())), preferred_element_type=F32)


def split(x):
    high = x.astype(BF16)
    return high, (x - high.astype(F32)).astype(BF16)


def kernel(
    ctx_n, head_n, width,
    q_hbm, k_hbm, v_hbm, ld_hbm, gain_hbm, up_hbm,
    dq_out, dk_out, dv_out,
    q, k, v, ld, gain, up,
    mix, dec, att, grad, wq, cum, cum_rows, dkp, dvp, dq, dk, dv,
    f_send, f_recv, f_tsend, f_trecv, f_pre,
    b_send, b_recv, b_tsend, b_trecv, b_pre,
    z_send, z_recv, levels,
    in_sem, out_sem,
    fs_sem, fr_sem, fts_sem, ftr_sem, fps_sem, fpr_sem,
    bs_sem, br_sem, bts_sem, btr_sem, bps_sem, bpr_sem,
    zs_sem, zr_sem, ls_sem, lr_sem,
):
    tokens = q.shape[0]
    heads = q.shape[1] // DIM
    half = heads // 2
    bits = ctx_n.bit_length() - 1
    bits_x = (bits - 1) // 2
    chips_x = 2**bits_x
    tiles = tokens // TILE
    me = lax.axis_index("ctx")
    zed = lax.axis_index("head")
    core = lax.rem(me, 2)
    own = core * half
    bit_values = [lax.rem(me // (2**b), 2) for b in range(bits)]
    partners = [me + (2**b) * (1 - 2 * bit_values[b]) for b in range(bits)]

    loads = []
    for i, (src, dst) in enumerate(
        ((ld_hbm, ld), (k_hbm, k), (v_hbm, v), (q_hbm, q), (gain_hbm, gain), (up_hbm, up))
    ):
        load = pltpu.make_async_copy(src, dst, in_sem.at[i])
        load.start()
        loads.append(load)
    load_ld, load_k, load_v, load_q, load_gain, load_up = loads

    barrier = pltpu.get_barrier_semaphore()
    for d in range(1, ctx_n):
        pl.semaphore_signal(
            barrier, inc=1, device_id=(lax.rem(me + d, ctx_n), zed), device_id_type=MESH
        )
    for d in range(1, head_n):
        pl.semaphore_signal(
            barrier, inc=1, device_id=(me, lax.rem(zed + d, head_n)), device_id_type=MESH
        )

    load_ld.wait()
    steps = jnp.pad(ld[...], ((0, 8 - heads), (0, 0)))
    row_id = lax.broadcasted_iota(jnp.int32, (tokens, tokens), 0)
    col_id = lax.broadcasted_iota(jnp.int32, (tokens, tokens), 1)
    until = jnp.where(row_id <= col_id, 1.0, 0.0).astype(BF16)
    top = steps.astype(BF16).astype(F32)
    rest = (steps - top).astype(BF16).astype(F32)
    parts = jnp.concatenate([top, rest, steps - top - rest, jnp.zeros_like(steps)], axis=0)
    sums = dot(parts.astype(BF16), until, (1, 0))
    rows_cum = sums[:8] + (sums[8:16] + sums[16:24])
    cum_rows[...] = rows_cum
    cum[...] = jnp.concatenate([rows_cum, jnp.zeros((DIM - 8, tokens), F32)], axis=0).T

    levels[me] = jnp.broadcast_to(rows_cum[:, tokens - 1 :], (8, DIM))
    pl.semaphore_wait(barrier, ctx_n + head_n - 2)
    level_copies = []
    for d in range(1, ctx_n):
        copy = pltpu.make_async_remote_copy(
            src_ref=levels.at[me], dst_ref=levels.at[me],
            send_sem=ls_sem.at[d - 1], recv_sem=lr_sem.at[d - 1],
            device_id=(lax.rem(me + d, ctx_n), zed), device_id_type=MESH,
        )
        copy.start()
        level_copies.append(copy)

    def columns(h):
        return slice(h * DIM, (h + 1) * DIM)

    def cum_column(h):
        return cum[:, h : h + 1]

    def total(h):
        return cum[tokens - 1 : tokens, h : h + 1]

    diagonal = lax.broadcasted_iota(jnp.int32, (TILE, TILE), 0) >= lax.broadcasted_iota(
        jnp.int32, (TILE, TILE), 1
    )

    def exchange(rev, send, recv, tsend, trecv, pre, ss, rs, tss, trs, pss, prs):
        pending = []
        spot = ctx_n - 1 - me if rev else me
        chip = spot // 2
        row_start = chip - lax.rem(chip, chips_x)

        def remote(src, dst, s_sem, r_sem, b):
            copy = pltpu.make_async_remote_copy(
                src_ref=src, dst_ref=dst, send_sem=s_sem, recv_sem=r_sem,
                device_id=(partners[b], zed), device_id_type=MESH,
            )
            copy.start()
            pending.append(copy)
            return copy

        def span(first, last, o):
            total_level = jnp.zeros((1, DIM), F32)
            for j in range(ctx_n):
                place = (ctx_n - 1 - j if rev else j) // 2
                inside = jnp.logical_and(first <= place, place < last)
                total_level = total_level + jnp.where(inside, levels[j, pl.ds(o, 1), :], 0.0)
            return jnp.exp(total_level)

        def is_upper(b):
            return lax.rem(spot // (2**b), 2) == 1

        first = []

        def post(h, value):
            send[h] = value
            first.append(remote(send.at[h], recv.at[h], ss.at[h], rs.at[h], 0))

        def slot_of(b, i, second):
            return ((b - 1) * half + i) * 2 + second

        copies = {}

        def publish(b, i, value, second=0):
            slot = slot_of(b, i, second)
            tsend[slot] = value
            copies[b, i, second] = remote(
                tsend.at[slot], trecv.at[slot], tss.at[slot], trs.at[slot], b
            )

        def arrived(b, i, second=0):
            copies[b, i, second].wait_recv()
            return trecv[slot_of(b, i, second)]

        def finish_head(i, value):
            pre[own + i] = value
            copies["pre", i] = remote(pre.at[own + i], pre.at[own + i], pss.at[i], prs.at[i], 0)

        def pair(i):
            o = own + i
            first_level = jnp.exp(levels[me, pl.ds(o, 1), :])
            other_level = jnp.exp(levels[partners[0], pl.ds(o, 1), :])
            upper = is_upper(0)
            return send[o] * jnp.where(upper, 1.0, other_level) + recv[o] * jnp.where(
                upper, first_level, 1.0
            )

        def straight(i):
            o = own + i
            value = pair(i)
            publish(1, i, value)
            yield
            before = jnp.zeros((DIM, DIM), F32)
            for b in range(1, bits):
                size = 2 ** (b - 1)
                upper = is_upper(b)
                other = arrived(b, i)
                group = chip - lax.rem(chip, size)
                before = before + jnp.where(upper, span(group, chip, o), 0.0) * other
                if b + 1 < bits:
                    upper_group = jnp.where(upper, group, group + size)
                    faded = span(upper_group, upper_group + size, o)
                    value = value * jnp.where(upper, 1.0, faded) + other * jnp.where(
                        upper, faded, 1.0
                    )
                    publish(b + 1, i, value)
                    yield
            finish_head(i, before)
            yield

        def crossed(i):
            o = own + i
            value = pair(i)
            column = value * span(chip + 1, row_start + chips_x, o)
            publish(bits_x + 1, i, column)
            yield
            above = jnp.zeros((DIM, DIM), F32)
            for b in range(bits_x + 1, bits):
                size = 2 ** (b - 1)
                upper = is_upper(b)
                other = arrived(b, i)
                group = chip - lax.rem(chip, size)
                above = above + jnp.where(upper, span(group, row_start, o), 0.0) * other
                if b + 1 < bits:
                    upper_group = jnp.where(upper, group, group + size)
                    faded = span(upper_group, upper_group + size, o)
                    column = column * jnp.where(upper, 1.0, faded) + other * jnp.where(
                        upper, faded, 1.0
                    )
                    publish(b + 1, i, column)
                    yield
            before = jnp.zeros((DIM, DIM), F32)
            for b in range(1, bits_x + 1):
                size = 2 ** (b - 1)
                upper = is_upper(b)
                group = chip - lax.rem(chip, size)
                to_chip = jnp.where(upper, span(group, chip, o), 0.0)
                if b < bits_x:
                    publish(b, i, value)
                    publish(b, i, above, 1)
                    yield
                    other = arrived(b, i)
                    above = above + arrived(b, i, 1)
                    before = before + to_chip * other
                    upper_group = jnp.where(upper, group, group + size)
                    faded = span(upper_group, upper_group + size, o)
                    value = value * jnp.where(upper, 1.0, faded) + other * jnp.where(
                        upper, faded, 1.0
                    )
                else:
                    until_end = span(row_start, group + size, o)
                    publish(b, i, jnp.where(upper, above, until_end * above + value))
                    yield
                    other = arrived(b, i)
                    until_chip = span(row_start, chip, o)
                    before = before + until_chip * above
                    before = before + jnp.where(upper, to_chip, until_chip) * other
            finish_head(i, before)
            yield

        routes = [straight(i) if i % 2 == 0 else crossed(i) for i in range(half)]

        def advance():
            for route in routes:
                next(route)

        def begin():
            for copy in first:
                copy.wait_recv()
            advance()

        def finish():
            for i in range(half):
                copies["pre", i].wait_recv()
            for copy in pending:
                copy.wait_send()

        def result(h):
            outside = pre[h]
            level = jnp.exp(levels[partners[0], h : h + 1, :])
            return jnp.where(is_upper(0), outside * level + recv[h], outside)

        return post, [begin] + [advance] * (bits - 1) + [finish], result

    post, stages, start_state = exchange(
        False, f_send, f_recv, f_tsend, f_trecv, f_pre,
        fs_sem, fr_sem, fts_sem, ftr_sem, fps_sem, fpr_sem,
    )

    load_k.wait()
    load_v.wait()
    for h in range(heads):
        ending = jnp.exp(total(h) - cum_column(h))
        weighted_keys = (k[:, columns(h)].astype(F32) * ending).astype(BF16)
        value = dot(weighted_keys, v[:, columns(h)], (0, 0))
        post(h, value)

    load_q.wait()

    def forward(h):
        for i in range(tiles):
            rows = slice(i * TILE, (i + 1) * TILE)
            total_rows = None
            for j in range(i + 1):
                sources = slice(j * TILE, (j + 1) * TILE)
                scores = dot(q[rows, columns(h)], k[sources, columns(h)], (1, 1))
                spread = cum[rows, h : h + 1] - cum_rows[h : h + 1, sources]
                if i == j:
                    spread = jnp.where(diagonal, spread, -1e30)
                decays = jnp.exp(spread)
                dec[h, rows, sources] = decays
                mixing = (scores * decays).astype(BF16)
                mix[h, rows, sources] = mixing
                part = dot(mixing, v[sources, columns(h)], (1, 0))
                total_rows = part if total_rows is None else total_rows + part
            att[rows, columns(h)] = total_rows

    def weigh_queries(h):
        wq[:, columns(h)] = (q[:, columns(h)].astype(F32) * jnp.exp(cum_column(h))).astype(BF16)

    def interleave(works, stages):
        for place in range(max(len(works), len(stages))):
            if place < len(works):
                works[place]()
            if place < len(stages):
                stages[place]()

    def forward_first():
        forward(0)
        for copy in level_copies:
            copy.wait()

    interleave(
        [forward_first] + [functools.partial(forward, h) for h in range(1, heads)], stages
    )

    load_gain.wait()
    load_up.wait()
    squares = None
    for h in range(heads):
        high, low = split(start_state(h))
        queries = q[:, columns(h)]
        carried = dot(
            jnp.concatenate([queries, queries], axis=1), jnp.concatenate([high, low], axis=0), (1, 0)
        )
        value = att[:, columns(h)] + jnp.exp(cum_column(h)) * carried
        att[:, columns(h)] = value
        scaled = gain[:, columns(h)] * up[:, columns(h)].astype(F32)
        square, cross = value * value, scaled * value
        squares = square if squares is None else squares + square
        crosses = cross if h == 0 else crosses + cross
    square_sum = jnp.sum(squares, axis=1, keepdims=True)
    cross_sum = jnp.sum(crosses, axis=1, keepdims=True)
    lane = lax.broadcasted_iota(jnp.int32, (tokens, DIM), 1)
    packed = jnp.where(lane == 0, square_sum, jnp.where(lane == 1, cross_sum, 0.0))
    z_send[...] = packed.T[:8]
    z_copies = []
    for d in range(1, head_n):
        copy = pltpu.make_async_remote_copy(
            src_ref=z_send, dst_ref=z_recv.at[d - 1],
            send_sem=zs_sem.at[d - 1], recv_sem=zr_sem.at[d - 1],
            device_id=(me, lax.rem(zed + d, head_n)), device_id_type=MESH,
        )
        copy.start()
        z_copies.append(copy)
    for h in range(heads):
        weigh_queries(h)
    sums = z_send[...]
    for d in range(1, head_n):
        z_copies[d - 1].wait_recv()
        sums = sums + z_recv[d - 1]
    full = jnp.concatenate([sums, jnp.zeros((DIM - 8, tokens), F32)], axis=0).T
    square_sum, cross_sum = full[:, 0:1], full[:, 1:2]
    inverse = lax.rsqrt(square_sum / width + EPSILON)
    factor = inverse * inverse * inverse * cross_sum / width

    post, stages, end_state = exchange(
        True, b_send, b_recv, b_tsend, b_trecv, b_pre,
        bs_sem, br_sem, bts_sem, btr_sem, bps_sem, bpr_sem,
    )
    for h in range(heads):
        scaled = gain[:, columns(h)] * up[:, columns(h)].astype(F32)
        value = (inverse * scaled - att[:, columns(h)] * factor).astype(BF16)
        grad[:, columns(h)] = value
        post(h, dot(wq[:, columns(h)], value, (0, 0)))
    for copy in z_copies:
        copy.wait_send()

    stores = []

    def store(i, h, src, dst):
        copy = pltpu.make_async_copy(
            src.at[:, columns(h)], dst.at[:, columns(h)], out_sem.at[i * heads + h]
        )
        copy.start()
        stores.append(copy)

    def backward(h):
        high, low = split(start_state(h))
        states = jnp.concatenate([high, low], axis=1)
        key_sums, value_sums = [None] * tiles, [None] * tiles
        for i in range(tiles):
            rows = slice(i * TILE, (i + 1) * TILE)
            grads = grad[rows, columns(h)]
            query_sum = jnp.exp(cum[rows, h : h + 1]) * dot(
                jnp.concatenate([grads, grads], axis=1), states, (1, 1)
            )
            for j in range(i + 1):
                sources = slice(j * TILE, (j + 1) * TILE)
                scores = dot(grads, v[sources, columns(h)], (1, 1))
                mixing = (scores * dec[h, rows, sources]).astype(BF16)
                query_sum = query_sum + dot(mixing, k[sources, columns(h)], (1, 0))
                key_part = dot(mixing, q[rows, columns(h)], (0, 0))
                value_part = dot(mix[h, rows, sources], grads, (0, 0))
                key_sums[j] = key_part if i == j else key_sums[j] + key_part
                value_sums[j] = value_part if i == j else value_sums[j] + value_part
            dq[rows, columns(h)] = query_sum.astype(BF16)
        store(0, h, dq, dq_out)
        for j in range(tiles):
            sources = slice(j * TILE, (j + 1) * TILE)
            dkp[sources, columns(h)] = key_sums[j]
            dvp[sources, columns(h)] = value_sums[j]

    interleave([functools.partial(backward, h) for h in range(heads)], stages)

    for h in range(heads):
        high, low = split(end_state(h))
        ending = jnp.exp(total(h) - cum_column(h))
        keys, values = k[:, columns(h)], v[:, columns(h)]
        key_carried = dot(
            jnp.concatenate([values, values], axis=1), jnp.concatenate([high, low], axis=1), (1, 1)
        )
        dk[:, columns(h)] = (ending * key_carried + dkp[:, columns(h)]).astype(BF16)
        store(1, h, dk, dk_out)
        value_carried = dot(
            jnp.concatenate([keys, keys], axis=1), jnp.concatenate([high, low], axis=0), (1, 0)
        )
        dv[:, columns(h)] = (ending * value_carried + dvp[:, columns(h)]).astype(BF16)
        store(2, h, dv, dv_out)
    for copy in stores:
        copy.wait()


def on_device(queries, keys, values, log_decay, gain, upstream):
    tokens, local = queries.shape
    heads = log_decay.shape[1]
    ctx_n, head_n = lax.axis_size("ctx"), lax.axis_size("head")
    slots = (ctx_n.bit_length() - 2) * heads
    half = heads // 2
    wide = (tokens, local)
    message = (heads, DIM, DIM)
    chip_message = (slots, DIM, DIM)
    states = [
        pltpu.VMEM(message, F32),
        pltpu.VMEM(message, F32),
        pltpu.VMEM(chip_message, F32),
        pltpu.VMEM(chip_message, F32),
        pltpu.VMEM((heads, DIM, DIM), F32),
    ]
    dma = pltpu.SemaphoreType.DMA
    state_sems = [
        dma((heads,)), dma((heads,)), dma((slots,)), dma((slots,)),
        dma((half,)), dma((half,)),
    ]
    anywhere = pl.BlockSpec(memory_space=pl.ANY)
    in_hbm = pl.BlockSpec(memory_space=pltpu.HBM)
    out = jax.ShapeDtypeStruct(wide, BF16)
    return pl.pallas_call(
        functools.partial(kernel, ctx_n, head_n, local * head_n),
        out_shape=(out, out, out),
        in_specs=[in_hbm] * 6,
        out_specs=(anywhere,) * 3,
        scratch_shapes=[
            pltpu.VMEM(wide, BF16),
            pltpu.VMEM(wide, BF16),
            pltpu.VMEM(wide, BF16),
            pltpu.VMEM((heads, tokens), F32),
            pltpu.VMEM((1, local), F32),
            pltpu.VMEM(wide, BF16),
            pltpu.VMEM((heads, tokens, tokens), BF16),
            pltpu.VMEM((heads, tokens, tokens), F32),
            pltpu.VMEM(wide, F32),
            pltpu.VMEM(wide, BF16),
            pltpu.VMEM(wide, BF16),
            pltpu.VMEM((tokens, DIM), F32),
            pltpu.VMEM((8, tokens), F32),
            pltpu.VMEM(wide, F32),
            pltpu.VMEM(wide, F32),
            pltpu.VMEM(wide, BF16),
            pltpu.VMEM(wide, BF16),
            pltpu.VMEM(wide, BF16),
            *states,
            *states,
            pltpu.VMEM((8, tokens), F32),
            pltpu.VMEM((head_n - 1, 8, tokens), F32),
            pltpu.VMEM((ctx_n, 8, DIM), F32),
            dma((6,)),
            dma((3 * heads,)),
            *state_sems,
            *state_sems,
            dma((head_n - 1,)),
            dma((head_n - 1,)),
            dma((ctx_n - 1,)),
            dma((ctx_n - 1,)),
        ],
        compiler_params=pltpu.CompilerParams(
            collective_id=0, has_side_effects=True, vmem_limit_bytes=60 * 2**20
        ),
        cost_estimate=pl.CostEstimate(
            flops=16 * heads * tokens * tokens * DIM,
            bytes_accessed=14 * tokens * local,
            transcendentals=heads * tokens * tokens,
        ),
    )(queries, keys, values, log_decay.T, gain.reshape(1, -1), upstream)


def solution(mesh):
    wide = P("ctx", "head")
    return jax.shard_map(
        on_device,
        mesh=mesh,
        in_specs=(wide, wide, wide, wide, P("head"), wide),
        out_specs=(wide, wide, wide),
        check_vma=False,
    )
```

```python
import functools

import jax
import jax.numpy as jnp
from jax import lax
from jax.experimental import pallas as pl
from jax.experimental.pallas import tpu as pltpu
from jax.sharding import PartitionSpec as P

DIM = 128
TILE = 256
COPIES = 4
EPSILON = 1e-06
MESH = pl.DeviceIdType.MESH
F32 = jnp.float32
BF16 = jnp.bfloat16


def dot(a, b, dims):
    return lax.dot_general(a, b, ((dims[:1], dims[1:]), ((), ())), preferred_element_type=F32)


def split(x):
    high = x.astype(BF16)
    return high, (x - high.astype(F32)).astype(BF16)


def kernel(
    ctx_n, head_n, width,
    q_hbm, k_hbm, v_hbm, ld_hbm, gain_hbm, up_hbm,
    dq_out, dk_out, dv_out,
    q, k, v, ld, gain, up,
    mix, dec, att, grad, wq, cum, cum_rows, dkp, dvp, dq, dk, dv,
    f_send, f_recv, f_tsend, f_trecv, f_pre,
    b_send, b_recv, b_tsend, b_trecv, b_pre,
    z_send, z_recv, levels,
    in_sem, out_sem,
    fs_sem, fr_sem, fts_sem, ftr_sem, fps_sem, fpr_sem,
    bs_sem, br_sem, bts_sem, btr_sem, bps_sem, bpr_sem,
    zs_sem, zr_sem, ls_sem, lr_sem,
):
    tokens = q.shape[0]
    heads = q.shape[1] // DIM
    half = heads // 2
    bits = ctx_n.bit_length() - 1
    bits_x = (bits - 1) // 2
    chips_x = 2**bits_x
    tiles = tokens // TILE
    me = lax.axis_index("ctx")
    zed = lax.axis_index("head")
    core = lax.rem(me, 2)
    own = core * half
    bit_values = [lax.rem(me // (2**b), 2) for b in range(bits)]
    partners = [me + (2**b) * (1 - 2 * bit_values[b]) for b in range(bits)]

    loads = []
    for i, (src, dst) in enumerate(
        ((ld_hbm, ld), (k_hbm, k), (v_hbm, v), (q_hbm, q), (gain_hbm, gain), (up_hbm, up))
    ):
        load = pltpu.make_async_copy(src, dst, in_sem.at[i])
        load.start()
        loads.append(load)
    load_ld, load_k, load_v, load_q, load_gain, load_up = loads

    barrier = pltpu.get_barrier_semaphore()
    for d in range(1, ctx_n):
        pl.semaphore_signal(
            barrier, inc=1, device_id=(lax.rem(me + d, ctx_n), zed), device_id_type=MESH
        )
    for d in range(1, head_n):
        pl.semaphore_signal(
            barrier, inc=1, device_id=(me, lax.rem(zed + d, head_n)), device_id_type=MESH
        )

    row_id = lax.broadcasted_iota(jnp.int32, (tokens, tokens), 0)
    col_id = lax.broadcasted_iota(jnp.int32, (tokens, tokens), 1)
    until = jnp.where(row_id <= col_id, 1.0, 0.0).astype(BF16)
    load_ld.wait()
    steps = jnp.pad(ld[...], ((0, 8 - heads), (0, 0)))
    top = steps.astype(BF16).astype(F32)
    rest = (steps - top).astype(BF16).astype(F32)
    parts = jnp.concatenate([top, rest, steps - top - rest, jnp.zeros_like(steps)], axis=0)
    sums = dot(parts.astype(BF16), until, (1, 0))
    rows_cum = sums[:8] + (sums[8:16] + sums[16:24])
    cum_rows[...] = rows_cum
    cum[...] = jnp.concatenate([rows_cum, jnp.zeros((DIM - 8, tokens), F32)], axis=0).T

    levels[me] = jnp.broadcast_to(rows_cum[:, tokens - 1 :], (8, DIM))
    pl.semaphore_wait(barrier, ctx_n + head_n - 2)
    level_copies = []
    for d in range(1, ctx_n):
        copy = pltpu.make_async_remote_copy(
            src_ref=levels.at[me], dst_ref=levels.at[me],
            send_sem=ls_sem.at[d - 1], recv_sem=lr_sem.at[d - 1],
            device_id=(lax.rem(me + d, ctx_n), zed), device_id_type=MESH,
        )
        copy.start()
        level_copies.append(copy)

    def columns(h):
        return slice(h * DIM, (h + 1) * DIM)

    def cum_column(h):
        return cum[:, h : h + 1]

    def total(h):
        return cum[tokens - 1 : tokens, h : h + 1]

    diagonal = lax.broadcasted_iota(jnp.int32, (TILE, TILE), 0) >= lax.broadcasted_iota(
        jnp.int32, (TILE, TILE), 1
    )

    def exchange(rev, send, recv, tsend, trecv, pre, ss, rs, tss, trs, pss, prs):
        pending = []
        spot = ctx_n - 1 - me if rev else me
        chip = spot // 2
        row_start = chip - lax.rem(chip, chips_x)

        def remote(src, dst, s_sem, r_sem, b):
            copy = pltpu.make_async_remote_copy(
                src_ref=src, dst_ref=dst, send_sem=s_sem, recv_sem=r_sem,
                device_id=(partners[b], zed), device_id_type=MESH,
            )
            copy.start()
            pending.append(copy)
            return copy

        def span(first, last, o):
            total_level = jnp.zeros((1, DIM), F32)
            for j in range(ctx_n):
                place = (ctx_n - 1 - j if rev else j) // 2
                inside = jnp.logical_and(first <= place, place < last)
                total_level = total_level + jnp.where(inside, levels[j, pl.ds(o, 1), :], 0.0)
            return jnp.exp(total_level)

        def is_upper(b):
            return lax.rem(spot // (2**b), 2) == 1

        first = []

        def post(h, value):
            send[h] = value
            first.append(remote(send.at[h], recv.at[h], ss.at[h], rs.at[h], 0))

        def slot_of(b, i, second):
            return ((b - 1) * half + i) * 2 + second

        copies = {}

        def publish(b, i, value, second=0):
            slot = slot_of(b, i, second)
            tsend[slot] = value
            copies[b, i, second] = remote(
                tsend.at[slot], trecv.at[slot], tss.at[slot], trs.at[slot], b
            )

        def arrived(b, i, second=0):
            copies[b, i, second].wait_recv()
            return trecv[slot_of(b, i, second)]

        def finish_head(i, value):
            pre[own + i] = value
            copies["pre", i] = remote(pre.at[own + i], pre.at[own + i], pss.at[i], prs.at[i], 0)

        def pair(i):
            o = own + i
            first_level = jnp.exp(levels[me, pl.ds(o, 1), :])
            other_level = jnp.exp(levels[partners[0], pl.ds(o, 1), :])
            upper = is_upper(0)
            return send[o] * jnp.where(upper, 1.0, other_level) + recv[o] * jnp.where(
                upper, first_level, 1.0
            )

        def straight(i):
            o = own + i
            value = pair(i)
            publish(1, i, value)
            yield
            before = jnp.zeros((DIM, DIM), F32)
            for b in range(1, bits):
                size = 2 ** (b - 1)
                upper = is_upper(b)
                other = arrived(b, i)
                group = chip - lax.rem(chip, size)
                before = before + jnp.where(upper, span(group, chip, o), 0.0) * other
                if b + 1 < bits:
                    upper_group = jnp.where(upper, group, group + size)
                    faded = span(upper_group, upper_group + size, o)
                    value = value * jnp.where(upper, 1.0, faded) + other * jnp.where(
                        upper, faded, 1.0
                    )
                    publish(b + 1, i, value)
                    yield
            finish_head(i, before)
            yield

        def crossed(i):
            o = own + i
            value = pair(i)
            column = value * span(chip + 1, row_start + chips_x, o)
            publish(bits_x + 1, i, column)
            yield
            above = jnp.zeros((DIM, DIM), F32)
            for b in range(bits_x + 1, bits):
                size = 2 ** (b - 1)
                upper = is_upper(b)
                other = arrived(b, i)
                group = chip - lax.rem(chip, size)
                above = above + jnp.where(upper, span(group, row_start, o), 0.0) * other
                if b + 1 < bits:
                    upper_group = jnp.where(upper, group, group + size)
                    faded = span(upper_group, upper_group + size, o)
                    column = column * jnp.where(upper, 1.0, faded) + other * jnp.where(
                        upper, faded, 1.0
                    )
                    publish(b + 1, i, column)
                    yield
            before = jnp.zeros((DIM, DIM), F32)
            for b in range(1, bits_x + 1):
                size = 2 ** (b - 1)
                upper = is_upper(b)
                group = chip - lax.rem(chip, size)
                to_chip = jnp.where(upper, span(group, chip, o), 0.0)
                if b < bits_x:
                    publish(b, i, value)
                    publish(b, i, above, 1)
                    yield
                    other = arrived(b, i)
                    above = above + arrived(b, i, 1)
                    before = before + to_chip * other
                    upper_group = jnp.where(upper, group, group + size)
                    faded = span(upper_group, upper_group + size, o)
                    value = value * jnp.where(upper, 1.0, faded) + other * jnp.where(
                        upper, faded, 1.0
                    )
                else:
                    until_end = span(row_start, group + size, o)
                    publish(b, i, jnp.where(upper, above, until_end * above + value))
                    yield
                    other = arrived(b, i)
                    until_chip = span(row_start, chip, o)
                    before = before + until_chip * above
                    before = before + jnp.where(upper, to_chip, until_chip) * other
            finish_head(i, before)
            yield

        routes = [straight(i) if i % 2 == 0 else crossed(i) for i in range(half)]

        def advance():
            for route in routes:
                next(route)

        def begin():
            for copy in first:
                copy.wait_recv()
            advance()

        def finish():
            for i in range(half):
                copies["pre", i].wait_recv()
            for copy in pending:
                copy.wait_send()

        def result(h):
            outside = pre[h]
            level = jnp.exp(levels[partners[0], h : h + 1, :])
            return jnp.where(is_upper(0), outside * level + recv[h], outside)

        return post, [begin] + [advance] * (bits - 1) + [finish], result

    post, stages, start_state = exchange(
        False, f_send, f_recv, f_tsend, f_trecv, f_pre,
        fs_sem, fr_sem, fts_sem, ftr_sem, fps_sem, fpr_sem,
    )

    load_k.wait()
    load_v.wait()
    for h in range(heads):
        row = cum_rows[h : h + 1, :]
        turned = k[:, columns(h)].T.astype(F32)
        weighted_keys = (turned * jnp.exp(row[:, tokens - 1 :] - row)).astype(BF16)
        post(h, dot(weighted_keys, v[:, columns(h)], (1, 0)))

    load_q.wait()

    def forward(h, i):
        rows = slice(i * TILE, (i + 1) * TILE)
        total_rows = None
        for j in range(i + 1):
            sources = slice(j * TILE, (j + 1) * TILE)
            scores = dot(q[rows, columns(h)], k[sources, columns(h)], (1, 1))
            spread = cum[rows, h : h + 1] - cum_rows[h : h + 1, sources]
            if i == j:
                spread = jnp.where(diagonal, spread, -1e30)
            decays = jnp.exp(spread)
            dec[h, rows, sources] = decays
            mixing = (scores * decays).astype(BF16)
            mix[h, sources, rows] = mixing.T
            part = dot(mixing, v[sources, columns(h)], (1, 0))
            total_rows = part if total_rows is None else total_rows + part
        att[rows, columns(h)] = total_rows

    def weigh_queries():
        for h in range(heads):
            turned = q[:, columns(h)].T.astype(F32)
            wq[columns(h), :] = (turned * jnp.exp(cum_rows[h : h + 1, :])).astype(BF16)

    def units(work):
        return [functools.partial(work, h, i) for h in range(heads) for i in range(tiles)]

    def interleave(works, stages):
        for place, stage in enumerate(stages):
            for work in works[place] if place < len(works) else ():
                work()
            stage()

    def receive_levels():
        for copy in level_copies:
            copy.wait()

    parts = units(forward)
    interleave([parts[:2] + [receive_levels], parts[2:5], parts[5:], [weigh_queries]], stages)

    load_gain.wait()
    load_up.wait()
    squares = None
    for h in range(heads):
        high, low = split(start_state(h))
        queries = q[:, columns(h)]
        carried = dot(
            jnp.concatenate([queries, queries], axis=1), jnp.concatenate([high, low], axis=0), (1, 0)
        )
        value = att[:, columns(h)] + jnp.exp(cum_column(h)) * carried
        att[:, columns(h)] = value
        scaled = gain[:, columns(h)] * up[:, columns(h)].astype(F32)
        square, cross = value * value, scaled * value
        squares = square if squares is None else squares + square
        crosses = cross if h == 0 else crosses + cross
    square_sum = jnp.sum(squares, axis=1, keepdims=True)
    cross_sum = jnp.sum(crosses, axis=1, keepdims=True)
    lane = lax.broadcasted_iota(jnp.int32, (tokens, DIM), 1)
    packed = jnp.where(lane == 0, square_sum, jnp.where(lane == 1, cross_sum, 0.0))
    z_send[...] = packed.T[:2]
    z_copies = []
    for d in range(1, head_n):
        copy = pltpu.make_async_remote_copy(
            src_ref=z_send, dst_ref=z_recv.at[d - 1],
            send_sem=zs_sem.at[d - 1], recv_sem=zr_sem.at[d - 1],
            device_id=(me, lax.rem(zed + d, head_n)), device_id_type=MESH,
        )
        copy.start()
        z_copies.append(copy)
    sums = z_send[...]
    for d in range(1, head_n):
        z_copies[d - 1].wait_recv()
        sums = sums + z_recv[d - 1]
    full = jnp.concatenate([sums, jnp.zeros((DIM - 2, tokens), F32)], axis=0).T
    square_sum, cross_sum = full[:, 0:1], full[:, 1:2]
    inverse = lax.rsqrt(square_sum / width + EPSILON)
    factor = inverse * inverse * inverse * cross_sum / width

    post, stages, end_state = exchange(
        True, b_send, b_recv, b_tsend, b_trecv, b_pre,
        bs_sem, br_sem, bts_sem, btr_sem, bps_sem, bpr_sem,
    )
    for h in range(heads):
        scaled = gain[:, columns(h)] * up[:, columns(h)].astype(F32)
        value = (inverse * scaled - att[:, columns(h)] * factor).astype(BF16)
        grad[:, columns(h)] = value
        post(h, dot(wq[columns(h), :], value, (1, 0)))
    for copy in z_copies:
        copy.wait_send()

    stores = []

    def store(i, h, src, dst):
        copy = pltpu.make_async_copy(
            src.at[:, columns(h)], dst.at[:, columns(h)], out_sem.at[i * heads + h]
        )
        copy.start()
        stores.append(copy)

    def backward(h, i):
        high, low = split(start_state(h))
        states = jnp.concatenate([high, low], axis=1)
        rows = slice(i * TILE, (i + 1) * TILE)
        grads = grad[rows, columns(h)]
        query_sum = jnp.exp(cum[rows, h : h + 1]) * dot(
            jnp.concatenate([grads, grads], axis=1), states, (1, 1)
        )
        for j in range(i + 1):
            sources = slice(j * TILE, (j + 1) * TILE)
            scores = dot(grads, v[sources, columns(h)], (1, 1))
            mixing = (scores * dec[h, rows, sources]).astype(BF16)
            query_sum = query_sum + dot(mixing, k[sources, columns(h)], (1, 0))
            key_part = dot(mixing, q[rows, columns(h)], (0, 0))
            value_part = dot(mix[h, sources, rows], grads, (1, 0))
            if i == j:
                dkp[sources, columns(h)] = key_part
                dvp[sources, columns(h)] = value_part
            else:
                dkp[sources, columns(h)] += key_part
                dvp[sources, columns(h)] += value_part
        dq[rows, columns(h)] = query_sum.astype(BF16)
        if i == tiles - 1:
            store(0, h, dq, dq_out)

    parts = units(backward)
    interleave([parts[:2], parts[2:5], parts[5:7], parts[7:]], stages)

    for h in range(heads):
        high, low = split(end_state(h))
        ending = jnp.exp(total(h) - cum_column(h))
        keys, values = k[:, columns(h)], v[:, columns(h)]
        key_carried = dot(
            jnp.concatenate([values, values], axis=1), jnp.concatenate([high, low], axis=1), (1, 1)
        )
        dk[:, columns(h)] = (ending * key_carried + dkp[:, columns(h)]).astype(BF16)
        store(1, h, dk, dk_out)
        value_carried = dot(
            jnp.concatenate([keys, keys], axis=1), jnp.concatenate([high, low], axis=0), (1, 0)
        )
        dv[:, columns(h)] = (ending * value_carried + dvp[:, columns(h)]).astype(BF16)
        store(2, h, dv, dv_out)
    for copy in stores:
        copy.wait()


def hand_over(*refs):
    count = (len(refs) - 1) // 2
    sem = refs[-1]
    copies = []
    for i in range(count):
        size = refs[i].shape[0] // COPIES
        for part in range(COPIES):
            rows = pl.ds(part * size, size)
            copy = pltpu.make_async_copy(
                refs[i].at[rows], refs[count + i].at[rows], sem.at[i * COPIES + part]
            )
            copy.start()
            copies.append(copy)
    for copy in copies:
        copy.wait()


def on_device(queries, keys, values, log_decay, gain, upstream):
    tokens, local = queries.shape
    heads = log_decay.shape[1]
    ctx_n, head_n = lax.axis_size("ctx"), lax.axis_size("head")
    slots = (ctx_n.bit_length() - 2) * heads
    half = heads // 2
    wide = (tokens, local)
    message = (heads, DIM, DIM)
    chip_message = (slots, DIM, DIM)
    states = [
        pltpu.VMEM(message, F32),
        pltpu.VMEM(message, F32),
        pltpu.VMEM(chip_message, F32),
        pltpu.VMEM(chip_message, F32),
        pltpu.VMEM((heads, DIM, DIM), F32),
    ]
    dma = pltpu.SemaphoreType.DMA
    state_sems = [
        dma((heads,)), dma((heads,)), dma((slots,)), dma((slots,)),
        dma((half,)), dma((half,)),
    ]
    anywhere = pl.BlockSpec(memory_space=pl.ANY)
    in_hbm = pl.BlockSpec(memory_space=pltpu.HBM)
    out = jax.ShapeDtypeStruct(wide, BF16)
    results = pl.pallas_call(
        functools.partial(kernel, ctx_n, head_n, local * head_n),
        out_shape=(out, out, out),
        in_specs=[in_hbm] * 6,
        out_specs=(anywhere,) * 3,
        scratch_shapes=[
            pltpu.VMEM(wide, BF16),
            pltpu.VMEM(wide, BF16),
            pltpu.VMEM(wide, BF16),
            pltpu.VMEM((heads, tokens), F32),
            pltpu.VMEM((1, local), F32),
            pltpu.VMEM(wide, BF16),
            pltpu.VMEM((heads, tokens, tokens), BF16),
            pltpu.VMEM((heads, tokens, tokens), F32),
            pltpu.VMEM(wide, F32),
            pltpu.VMEM(wide, BF16),
            pltpu.VMEM((local, tokens), BF16),
            pltpu.VMEM((tokens, DIM), F32),
            pltpu.VMEM((8, tokens), F32),
            pltpu.VMEM(wide, F32),
            pltpu.VMEM(wide, F32),
            pltpu.VMEM(wide, BF16),
            pltpu.VMEM(wide, BF16),
            pltpu.VMEM(wide, BF16),
            *states,
            *states,
            pltpu.VMEM((2, tokens), F32),
            pltpu.VMEM((head_n - 1, 2, tokens), F32),
            pltpu.VMEM((ctx_n, 8, DIM), F32),
            dma((6,)),
            dma((3 * heads,)),
            *state_sems,
            *state_sems,
            dma((head_n - 1,)),
            dma((head_n - 1,)),
            dma((ctx_n - 1,)),
            dma((ctx_n - 1,)),
        ],
        compiler_params=pltpu.CompilerParams(
            collective_id=0, has_side_effects=True, vmem_limit_bytes=52 * 2**20
        ),
        cost_estimate=pl.CostEstimate(
            flops=16 * heads * tokens * tokens * DIM,
            bytes_accessed=14 * tokens * local,
            transcendentals=heads * tokens * tokens,
        ),
    )(queries, keys, values, log_decay.T, gain.reshape(1, -1), upstream)
    return pl.pallas_call(
        hand_over,
        out_shape=(out, out, out),
        in_specs=[anywhere] * 3,
        out_specs=(anywhere,) * 3,
        scratch_shapes=[dma((3 * COPIES,))],
    )(*results)


def solution(mesh):
    wide = P("ctx", "head")
    return jax.shard_map(
        on_device,
        mesh=mesh,
        in_specs=(wide, wide, wide, wide, P("head"), wide),
        out_specs=(wide, wide, wide),
        check_vma=False,
    )
```

```python
import functools

import jax
import jax.numpy as jnp
from jax import lax
from jax.experimental import pallas as pl
from jax.experimental.pallas import tpu as pltpu
from jax.sharding import PartitionSpec as P

DIM = 128
TILE = 256
COPIES = 4
EPSILON = 1e-06
MESH = pl.DeviceIdType.MESH
F32 = jnp.float32
BF16 = jnp.bfloat16


def dot(a, b, dims):
    return lax.dot_general(a, b, ((dims[:1], dims[1:]), ((), ())), preferred_element_type=F32)


def split(x):
    high = x.astype(BF16)
    return high, (x - high.astype(F32)).astype(BF16)


def kernel(
    ctx_n, head_n, width,
    q_hbm, k_hbm, v_hbm, ld_hbm, gain_hbm, up_hbm,
    dq, dk, dv,
    q, k, v, ld, gain, up,
    mix, dec, att, grad, wq, cum, cum_rows, dkp, dvp,
    f_send, f_recv, f_tsend, f_trecv, f_pre,
    b_send, b_recv, b_tsend, b_trecv, b_pre,
    z_send, z_recv, levels,
    in_sem,
    fs_sem, fr_sem, fts_sem, ftr_sem, fps_sem, fpr_sem,
    bs_sem, br_sem, bts_sem, btr_sem, bps_sem, bpr_sem,
    zs_sem, zr_sem, ls_sem, lr_sem,
):
    tokens = q.shape[0]
    heads = q.shape[1] // DIM
    half = heads // 2
    bits = ctx_n.bit_length() - 1
    bits_x = (bits - 1) // 2
    chips_x = 2**bits_x
    tiles = tokens // TILE
    me = lax.axis_index("ctx")
    zed = lax.axis_index("head")
    core = lax.rem(me, 2)
    own = core * half
    bit_values = [lax.rem(me // (2**b), 2) for b in range(bits)]
    partners = [me + (2**b) * (1 - 2 * bit_values[b]) for b in range(bits)]

    loads = []
    for i, (src, dst) in enumerate(
        ((ld_hbm, ld), (k_hbm, k), (v_hbm, v), (q_hbm, q), (gain_hbm, gain), (up_hbm, up))
    ):
        load = pltpu.make_async_copy(src, dst, in_sem.at[i])
        load.start()
        loads.append(load)
    load_ld, load_k, load_v, load_q, load_gain, load_up = loads

    barrier = pltpu.get_barrier_semaphore()
    for d in range(1, ctx_n):
        pl.semaphore_signal(
            barrier, inc=1, device_id=(lax.rem(me + d, ctx_n), zed), device_id_type=MESH
        )
    for d in range(1, head_n):
        pl.semaphore_signal(
            barrier, inc=1, device_id=(me, lax.rem(zed + d, head_n)), device_id_type=MESH
        )

    row_id = lax.broadcasted_iota(jnp.int32, (tokens, tokens), 0)
    col_id = lax.broadcasted_iota(jnp.int32, (tokens, tokens), 1)
    until = jnp.where(row_id <= col_id, 1.0, 0.0).astype(BF16)
    load_ld.wait()
    steps = jnp.pad(ld[...], ((0, 8 - heads), (0, 0)))
    top = steps.astype(BF16).astype(F32)
    rest = (steps - top).astype(BF16).astype(F32)
    parts = jnp.concatenate([top, rest, steps - top - rest, jnp.zeros_like(steps)], axis=0)
    sums = dot(parts.astype(BF16), until, (1, 0))
    rows_cum = sums[:8] + (sums[8:16] + sums[16:24])
    cum_rows[...] = rows_cum
    cum[...] = jnp.concatenate([rows_cum, jnp.zeros((DIM - 8, tokens), F32)], axis=0).T

    levels[me] = jnp.broadcast_to(rows_cum[:, tokens - 1 :], (8, DIM))
    pl.semaphore_wait(barrier, ctx_n + head_n - 2)
    level_copies = []
    for d in range(1, ctx_n):
        copy = pltpu.make_async_remote_copy(
            src_ref=levels.at[me], dst_ref=levels.at[me],
            send_sem=ls_sem.at[d - 1], recv_sem=lr_sem.at[d - 1],
            device_id=(lax.rem(me + d, ctx_n), zed), device_id_type=MESH,
        )
        copy.start()
        level_copies.append(copy)

    def columns(h):
        return slice(h * DIM, (h + 1) * DIM)

    def cum_column(h):
        return cum[:, h : h + 1]

    def total(h):
        return cum[tokens - 1 : tokens, h : h + 1]

    diagonal = lax.broadcasted_iota(jnp.int32, (TILE, TILE), 0) >= lax.broadcasted_iota(
        jnp.int32, (TILE, TILE), 1
    )

    def exchange(rev, send, recv, tsend, trecv, pre, ss, rs, tss, trs, pss, prs):
        pending = []
        spot = ctx_n - 1 - me if rev else me
        chip = spot // 2
        row_start = chip - lax.rem(chip, chips_x)

        def remote(src, dst, s_sem, r_sem, b):
            copy = pltpu.make_async_remote_copy(
                src_ref=src, dst_ref=dst, send_sem=s_sem, recv_sem=r_sem,
                device_id=(partners[b], zed), device_id_type=MESH,
            )
            copy.start()
            pending.append(copy)
            return copy

        def span(first, last, o):
            total_level = jnp.zeros((1, DIM), F32)
            for j in range(ctx_n):
                place = (ctx_n - 1 - j if rev else j) // 2
                inside = jnp.logical_and(first <= place, place < last)
                total_level = total_level + jnp.where(inside, levels[j, pl.ds(o, 1), :], 0.0)
            return jnp.exp(total_level)

        def is_upper(b):
            return lax.rem(spot // (2**b), 2) == 1

        first = []

        def post(h, value):
            send[h] = value
            first.append(remote(send.at[h], recv.at[h], ss.at[h], rs.at[h], 0))

        def slot_of(b, i, second):
            return ((b - 1) * half + i) * 2 + second

        copies = {}

        def publish(b, i, value, second=0):
            slot = slot_of(b, i, second)
            tsend[slot] = value
            copies[b, i, second] = remote(
                tsend.at[slot], trecv.at[slot], tss.at[slot], trs.at[slot], b
            )

        def arrived(b, i, second=0):
            copies[b, i, second].wait_recv()
            return trecv[slot_of(b, i, second)]

        def finish_head(i, value):
            pre[own + i] = value
            copies["pre", i] = remote(pre.at[own + i], pre.at[own + i], pss.at[i], prs.at[i], 0)

        def pair(i):
            o = own + i
            first_level = jnp.exp(levels[me, pl.ds(o, 1), :])
            other_level = jnp.exp(levels[partners[0], pl.ds(o, 1), :])
            upper = is_upper(0)
            return send[o] * jnp.where(upper, 1.0, other_level) + recv[o] * jnp.where(
                upper, first_level, 1.0
            )

        def straight(i):
            o = own + i
            value = pair(i)
            publish(1, i, value)
            yield
            before = jnp.zeros((DIM, DIM), F32)
            for b in range(1, bits):
                size = 2 ** (b - 1)
                upper = is_upper(b)
                other = arrived(b, i)
                group = chip - lax.rem(chip, size)
                before = before + jnp.where(upper, span(group, chip, o), 0.0) * other
                if b + 1 < bits:
                    upper_group = jnp.where(upper, group, group + size)
                    faded = span(upper_group, upper_group + size, o)
                    value = value * jnp.where(upper, 1.0, faded) + other * jnp.where(
                        upper, faded, 1.0
                    )
                    publish(b + 1, i, value)
                    yield
            finish_head(i, before)
            yield

        def crossed(i):
            o = own + i
            value = pair(i)
            column = value * span(chip + 1, row_start + chips_x, o)
            publish(bits_x + 1, i, column)
            yield
            above = jnp.zeros((DIM, DIM), F32)
            for b in range(bits_x + 1, bits):
                size = 2 ** (b - 1)
                upper = is_upper(b)
                other = arrived(b, i)
                group = chip - lax.rem(chip, size)
                above = above + jnp.where(upper, span(group, row_start, o), 0.0) * other
                if b + 1 < bits:
                    upper_group = jnp.where(upper, group, group + size)
                    faded = span(upper_group, upper_group + size, o)
                    column = column * jnp.where(upper, 1.0, faded) + other * jnp.where(
                        upper, faded, 1.0
                    )
                    publish(b + 1, i, column)
                    yield
            before = jnp.zeros((DIM, DIM), F32)
            for b in range(1, bits_x + 1):
                size = 2 ** (b - 1)
                upper = is_upper(b)
                group = chip - lax.rem(chip, size)
                to_chip = jnp.where(upper, span(group, chip, o), 0.0)
                if b < bits_x:
                    publish(b, i, value)
                    publish(b, i, above, 1)
                    yield
                    other = arrived(b, i)
                    above = above + arrived(b, i, 1)
                    before = before + to_chip * other
                    upper_group = jnp.where(upper, group, group + size)
                    faded = span(upper_group, upper_group + size, o)
                    value = value * jnp.where(upper, 1.0, faded) + other * jnp.where(
                        upper, faded, 1.0
                    )
                else:
                    until_end = span(row_start, group + size, o)
                    publish(b, i, jnp.where(upper, above, until_end * above + value))
                    yield
                    other = arrived(b, i)
                    until_chip = span(row_start, chip, o)
                    before = before + until_chip * above
                    before = before + jnp.where(upper, to_chip, until_chip) * other
            finish_head(i, before)
            yield

        routes = [straight(i) if i % 2 == 0 else crossed(i) for i in range(half)]

        def advance():
            for route in routes:
                next(route)

        def begin():
            for copy in first:
                copy.wait_recv()
            advance()

        def finish():
            for i in range(half):
                copies["pre", i].wait_recv()
            for copy in pending:
                copy.wait_send()

        def result(h):
            outside = pre[h]
            level = jnp.exp(levels[partners[0], h : h + 1, :])
            return jnp.where(is_upper(0), outside * level + recv[h], outside)

        return post, [begin] + [advance] * (bits - 1) + [finish], result

    post, stages, start_state = exchange(
        False, f_send, f_recv, f_tsend, f_trecv, f_pre,
        fs_sem, fr_sem, fts_sem, ftr_sem, fps_sem, fpr_sem,
    )

    load_k.wait()
    load_v.wait()
    for h in range(heads):
        row = cum_rows[h : h + 1, :]
        turned = k[:, columns(h)].T.astype(F32)
        weighted_keys = (turned * jnp.exp(row[:, tokens - 1 :] - row)).astype(BF16)
        post(h, dot(weighted_keys, v[:, columns(h)], (1, 0)))

    load_q.wait()

    def forward(h, i):
        rows = slice(i * TILE, (i + 1) * TILE)
        total_rows = None
        for j in range(i + 1):
            sources = slice(j * TILE, (j + 1) * TILE)
            scores = dot(q[rows, columns(h)], k[sources, columns(h)], (1, 1))
            spread = cum[rows, h : h + 1] - cum_rows[h : h + 1, sources]
            if i == j:
                spread = jnp.where(diagonal, spread, -1e30)
            decays = jnp.exp(spread)
            dec[h, rows, sources] = decays
            mixing = (scores * decays).astype(BF16)
            mix[h, sources, rows] = mixing.T
            part = dot(mixing, v[sources, columns(h)], (1, 0))
            total_rows = part if total_rows is None else total_rows + part
        att[rows, columns(h)] = total_rows

    def weigh_queries():
        for h in range(heads):
            turned = q[:, columns(h)].T.astype(F32)
            wq[columns(h), :] = (turned * jnp.exp(cum_rows[h : h + 1, :])).astype(BF16)

    def units(work):
        return [functools.partial(work, h, i) for h in range(heads) for i in range(tiles)]

    def interleave(works, stages):
        for place, stage in enumerate(stages):
            for work in works[place] if place < len(works) else ():
                work()
            stage()

    def receive_levels():
        for copy in level_copies:
            copy.wait()

    parts = units(forward)
    interleave([parts[:2] + [receive_levels], parts[2:5], parts[5:], [weigh_queries]], stages)

    load_gain.wait()
    load_up.wait()
    squares = None
    for h in range(heads):
        high, low = split(start_state(h))
        queries = q[:, columns(h)]
        carried = dot(
            jnp.concatenate([queries, queries], axis=1), jnp.concatenate([high, low], axis=0), (1, 0)
        )
        value = att[:, columns(h)] + jnp.exp(cum_column(h)) * carried
        att[:, columns(h)] = value
        scaled = gain[:, columns(h)] * up[:, columns(h)].astype(F32)
        square, cross = value * value, scaled * value
        squares = square if squares is None else squares + square
        crosses = cross if h == 0 else crosses + cross
    square_sum = jnp.sum(squares, axis=1, keepdims=True)
    cross_sum = jnp.sum(crosses, axis=1, keepdims=True)
    lane = lax.broadcasted_iota(jnp.int32, (tokens, DIM), 1)
    packed = jnp.where(lane == 0, square_sum, jnp.where(lane == 1, cross_sum, 0.0))
    z_send[...] = packed.T[:2]
    z_copies = []
    for d in range(1, head_n):
        copy = pltpu.make_async_remote_copy(
            src_ref=z_send, dst_ref=z_recv.at[d - 1],
            send_sem=zs_sem.at[d - 1], recv_sem=zr_sem.at[d - 1],
            device_id=(me, lax.rem(zed + d, head_n)), device_id_type=MESH,
        )
        copy.start()
        z_copies.append(copy)
    sums = z_send[...]
    for d in range(1, head_n):
        z_copies[d - 1].wait_recv()
        sums = sums + z_recv[d - 1]
    full = jnp.concatenate([sums, jnp.zeros((DIM - 2, tokens), F32)], axis=0).T
    square_sum, cross_sum = full[:, 0:1], full[:, 1:2]
    inverse = lax.rsqrt(square_sum / width + EPSILON)
    factor = inverse * inverse * inverse * cross_sum / width

    post, stages, end_state = exchange(
        True, b_send, b_recv, b_tsend, b_trecv, b_pre,
        bs_sem, br_sem, bts_sem, btr_sem, bps_sem, bpr_sem,
    )
    for h in range(heads):
        scaled = gain[:, columns(h)] * up[:, columns(h)].astype(F32)
        value = (inverse * scaled - att[:, columns(h)] * factor).astype(BF16)
        grad[:, columns(h)] = value
        post(h, dot(wq[columns(h), :], value, (1, 0)))
    for copy in z_copies:
        copy.wait_send()

    def backward(h, i):
        high, low = split(start_state(h))
        states = jnp.concatenate([high, low], axis=1)
        rows = slice(i * TILE, (i + 1) * TILE)
        grads = grad[rows, columns(h)]
        query_sum = jnp.exp(cum[rows, h : h + 1]) * dot(
            jnp.concatenate([grads, grads], axis=1), states, (1, 1)
        )
        for j in range(i + 1):
            sources = slice(j * TILE, (j + 1) * TILE)
            scores = dot(grads, v[sources, columns(h)], (1, 1))
            mixing = (scores * dec[h, rows, sources]).astype(BF16)
            query_sum = query_sum + dot(mixing, k[sources, columns(h)], (1, 0))
            key_part = dot(mixing, q[rows, columns(h)], (0, 0))
            value_part = dot(mix[h, sources, rows], grads, (1, 0))
            if i == j:
                dkp[sources, columns(h)] = key_part
                dvp[sources, columns(h)] = value_part
            else:
                dkp[sources, columns(h)] += key_part
                dvp[sources, columns(h)] += value_part
        dq[rows, columns(h)] = query_sum.astype(BF16)

    parts = units(backward)
    interleave([parts[:2], parts[2:5], parts[5:7], parts[7:]], stages)

    for h in range(heads):
        high, low = split(end_state(h))
        ending = jnp.exp(total(h) - cum_column(h))
        keys, values = k[:, columns(h)], v[:, columns(h)]
        key_carried = dot(
            jnp.concatenate([values, values], axis=1), jnp.concatenate([high, low], axis=1), (1, 1)
        )
        dk[:, columns(h)] = (ending * key_carried + dkp[:, columns(h)]).astype(BF16)
        value_carried = dot(
            jnp.concatenate([keys, keys], axis=1), jnp.concatenate([high, low], axis=0), (1, 0)
        )
        dv[:, columns(h)] = (ending * value_carried + dvp[:, columns(h)]).astype(BF16)


def hand_over(*refs):
    count = (len(refs) - 1) // 2
    sem = refs[-1]
    copies = []
    for i in range(count):
        size = refs[i].shape[0] // COPIES
        for part in range(COPIES):
            rows = pl.ds(part * size, size)
            copy = pltpu.make_async_copy(
                refs[i].at[rows], refs[count + i].at[rows], sem.at[i * COPIES + part]
            )
            copy.start()
            copies.append(copy)
    for copy in copies:
        copy.wait()


def on_device(queries, keys, values, log_decay, gain, upstream):
    tokens, local = queries.shape
    heads = log_decay.shape[1]
    ctx_n, head_n = lax.axis_size("ctx"), lax.axis_size("head")
    slots = (ctx_n.bit_length() - 2) * heads
    half = heads // 2
    wide = (tokens, local)
    message = (heads, DIM, DIM)
    chip_message = (slots, DIM, DIM)
    states = [
        pltpu.VMEM(message, F32),
        pltpu.VMEM(message, F32),
        pltpu.VMEM(chip_message, F32),
        pltpu.VMEM(chip_message, F32),
        pltpu.VMEM((heads, DIM, DIM), F32),
    ]
    dma = pltpu.SemaphoreType.DMA
    state_sems = [
        dma((heads,)), dma((heads,)), dma((slots,)), dma((slots,)),
        dma((half,)), dma((half,)),
    ]
    in_vmem = pl.BlockSpec(memory_space=pltpu.VMEM)
    in_hbm = pl.BlockSpec(memory_space=pltpu.HBM)
    out = jax.ShapeDtypeStruct(wide, BF16)
    results = pl.pallas_call(
        functools.partial(kernel, ctx_n, head_n, local * head_n),
        out_shape=(pltpu.VMEM(wide, BF16),) * 3,
        in_specs=[in_hbm] * 6,
        out_specs=(in_vmem,) * 3,
        scratch_shapes=[
            pltpu.VMEM(wide, BF16),
            pltpu.VMEM(wide, BF16),
            pltpu.VMEM(wide, BF16),
            pltpu.VMEM((heads, tokens), F32),
            pltpu.VMEM((1, local), F32),
            pltpu.VMEM(wide, BF16),
            pltpu.VMEM((heads, tokens, tokens), BF16),
            pltpu.VMEM((heads, tokens, tokens), F32),
            pltpu.VMEM(wide, F32),
            pltpu.VMEM(wide, BF16),
            pltpu.VMEM((local, tokens), BF16),
            pltpu.VMEM((tokens, DIM), F32),
            pltpu.VMEM((8, tokens), F32),
            pltpu.VMEM(wide, F32),
            pltpu.VMEM(wide, F32),
            *states,
            *states,
            pltpu.VMEM((2, tokens), F32),
            pltpu.VMEM((head_n - 1, 2, tokens), F32),
            pltpu.VMEM((ctx_n, 8, DIM), F32),
            dma((6,)),
            *state_sems,
            *state_sems,
            dma((head_n - 1,)),
            dma((head_n - 1,)),
            dma((ctx_n - 1,)),
            dma((ctx_n - 1,)),
        ],
        compiler_params=pltpu.CompilerParams(
            collective_id=0, has_side_effects=True, vmem_limit_bytes=60 * 2**20
        ),
        cost_estimate=pl.CostEstimate(
            flops=16 * heads * tokens * tokens * DIM,
            bytes_accessed=14 * tokens * local,
            transcendentals=heads * tokens * tokens,
        ),
    )(queries, keys, values, log_decay.T, gain.reshape(1, -1), upstream)
    return pl.pallas_call(
        hand_over,
        out_shape=(out, out, out),
        in_specs=[in_vmem] * 3,
        out_specs=(in_hbm,) * 3,
        scratch_shapes=[dma((3 * COPIES,))],
        compiler_params=pltpu.CompilerParams(vmem_limit_bytes=8 * 2**20),
    )(*results)


def solution(mesh):
    wide = P("ctx", "head")
    return jax.shard_map(
        on_device,
        mesh=mesh,
        in_specs=(wide, wide, wide, wide, P("head"), wide),
        out_specs=(wide, wide, wide),
        check_vma=False,
    )
```

```python
import functools

import jax
import jax.numpy as jnp
from jax import lax
from jax.experimental import pallas as pl
from jax.experimental.pallas import tpu as pltpu
from jax.sharding import PartitionSpec as P

DIM = 128
TILE = 256
COPIES = 4
EPSILON = 1e-06
MESH = pl.DeviceIdType.MESH
F32 = jnp.float32
BF16 = jnp.bfloat16


def dot(a, b, dims):
    return lax.dot_general(a, b, ((dims[:1], dims[1:]), ((), ())), preferred_element_type=F32)


def split(x):
    high = x.astype(BF16)
    return high, (x - high.astype(F32)).astype(BF16)


def kernel(
    ctx_n, head_n, width,
    q_hbm, k_hbm, v_hbm, ld_hbm, gain_hbm, up_hbm,
    dq, dk, dv,
    q, k, v, ld, gain, up,
    mix, dec, att, grad, wq, cum, cum_rows, dkp, dvp, start_factor, end_factor, states,
    f_send, f_recv, f_tsend, f_trecv, f_pre,
    b_send, b_recv, b_tsend, b_trecv, b_pre,
    z_send, z_recv, levels,
    in_sem,
    fs_sem, fr_sem, fts_sem, ftr_sem, fps_sem, fpr_sem,
    bs_sem, br_sem, bts_sem, btr_sem, bps_sem, bpr_sem,
    zs_sem, zr_sem, ls_sem, lr_sem,
):
    tokens = q.shape[0]
    heads = q.shape[1] // DIM
    half = heads // 2
    bits = ctx_n.bit_length() - 1
    bits_x = (bits - 1) // 2
    chips_x = 2**bits_x
    tiles = tokens // TILE
    me = lax.axis_index("ctx")
    zed = lax.axis_index("head")
    core = lax.rem(me, 2)
    own = core * half
    bit_values = [lax.rem(me // (2**b), 2) for b in range(bits)]
    partners = [me + (2**b) * (1 - 2 * bit_values[b]) for b in range(bits)]

    loads = []
    for i, (src, dst) in enumerate(
        ((ld_hbm, ld), (k_hbm, k), (v_hbm, v), (q_hbm, q), (gain_hbm, gain), (up_hbm, up))
    ):
        load = pltpu.make_async_copy(src, dst, in_sem.at[i])
        load.start()
        loads.append(load)
    load_ld, load_k, load_v, load_q, load_gain, load_up = loads

    barrier = pltpu.get_barrier_semaphore()
    for d in range(1, ctx_n):
        pl.semaphore_signal(
            barrier, inc=1, device_id=(lax.rem(me + d, ctx_n), zed), device_id_type=MESH
        )
    for d in range(1, head_n):
        pl.semaphore_signal(
            barrier, inc=1, device_id=(me, lax.rem(zed + d, head_n)), device_id_type=MESH
        )

    row_id = lax.broadcasted_iota(jnp.int32, (tokens, tokens), 0)
    col_id = lax.broadcasted_iota(jnp.int32, (tokens, tokens), 1)
    until = jnp.where(row_id <= col_id, 1.0, 0.0).astype(BF16)
    load_ld.wait()
    steps = jnp.pad(ld[...], ((0, 8 - heads), (0, 0)))
    top = steps.astype(BF16).astype(F32)
    rest = (steps - top).astype(BF16).astype(F32)
    parts = jnp.concatenate([top, rest, steps - top - rest, jnp.zeros_like(steps)], axis=0)
    sums = dot(parts.astype(BF16), until, (1, 0))
    rows_cum = sums[:8] + (sums[8:16] + sums[16:24])
    cum_rows[...] = rows_cum
    cum[...] = jnp.concatenate([rows_cum, jnp.zeros((DIM - 8, tokens), F32)], axis=0).T

    levels[me] = jnp.broadcast_to(rows_cum[:, tokens - 1 :], (8, DIM))
    pl.semaphore_wait(barrier, ctx_n + head_n - 2)
    level_copies = []
    for d in range(1, ctx_n):
        copy = pltpu.make_async_remote_copy(
            src_ref=levels.at[me], dst_ref=levels.at[me],
            send_sem=ls_sem.at[d - 1], recv_sem=lr_sem.at[d - 1],
            device_id=(lax.rem(me + d, ctx_n), zed), device_id_type=MESH,
        )
        copy.start()
        level_copies.append(copy)

    def columns(h):
        return slice(h * DIM, (h + 1) * DIM)

    diagonal = lax.broadcasted_iota(jnp.int32, (TILE, TILE), 0) >= lax.broadcasted_iota(
        jnp.int32, (TILE, TILE), 1
    )

    def exchange(rev, send, recv, tsend, trecv, pre, ss, rs, tss, trs, pss, prs):
        pending = []
        spot = ctx_n - 1 - me if rev else me
        chip = spot // 2
        row_start = chip - lax.rem(chip, chips_x)

        def remote(src, dst, s_sem, r_sem, b):
            copy = pltpu.make_async_remote_copy(
                src_ref=src, dst_ref=dst, send_sem=s_sem, recv_sem=r_sem,
                device_id=(partners[b], zed), device_id_type=MESH,
            )
            copy.start()
            pending.append(copy)
            return copy

        def span(first, last, o):
            total_level = jnp.zeros((1, DIM), F32)
            for j in range(ctx_n):
                place = (ctx_n - 1 - j if rev else j) // 2
                inside = jnp.logical_and(first <= place, place < last)
                total_level = total_level + jnp.where(inside, levels[j, pl.ds(o, 1), :], 0.0)
            return jnp.exp(total_level)

        def is_upper(b):
            return lax.rem(spot // (2**b), 2) == 1

        first = []

        def post(r, h, value):
            send[h] = value
            first.append(remote(send.at[h], recv.at[h], ss.at[r], rs.at[r], 0))

        def slot_of(b, i, second):
            return ((b - 1) * half + i) * 2 + second

        copies = {}

        def publish(b, i, value, second=0):
            slot = slot_of(b, i, second)
            tsend[slot] = value
            copies[b, i, second] = remote(
                tsend.at[slot], trecv.at[slot], tss.at[slot], trs.at[slot], b
            )

        def arrived(b, i, second=0):
            copies[b, i, second].wait_recv()
            return trecv[slot_of(b, i, second)]

        def finish_head(i, value):
            pre[own + i] = value
            copies["pre", i] = remote(pre.at[own + i], pre.at[own + i], pss.at[i], prs.at[i], 0)

        def pair(i):
            o = own + i
            first_level = jnp.exp(levels[me, pl.ds(o, 1), :])
            other_level = jnp.exp(levels[partners[0], pl.ds(o, 1), :])
            upper = is_upper(0)
            return send[o] * jnp.where(upper, 1.0, other_level) + recv[o] * jnp.where(
                upper, first_level, 1.0
            )

        def straight(i):
            o = own + i
            value = pair(i)
            publish(1, i, value)
            yield
            before = jnp.zeros((DIM, DIM), F32)
            for b in range(1, bits):
                size = 2 ** (b - 1)
                upper = is_upper(b)
                group = chip - lax.rem(chip, size)
                to_chip = jnp.where(upper, span(group, chip, o), 0.0)
                upper_group = jnp.where(upper, group, group + size)
                faded = span(upper_group, upper_group + size, o)
                other = arrived(b, i)
                before = before + to_chip * other
                if b + 1 < bits:
                    value = value * jnp.where(upper, 1.0, faded) + other * jnp.where(
                        upper, faded, 1.0
                    )
                    publish(b + 1, i, value)
                    yield
            finish_head(i, before)
            yield

        def crossed(i):
            o = own + i
            value = pair(i)
            column = value * span(chip + 1, row_start + chips_x, o)
            publish(bits_x + 1, i, column)
            yield
            above = jnp.zeros((DIM, DIM), F32)
            for b in range(bits_x + 1, bits):
                size = 2 ** (b - 1)
                upper = is_upper(b)
                group = chip - lax.rem(chip, size)
                to_row = jnp.where(upper, span(group, row_start, o), 0.0)
                upper_group = jnp.where(upper, group, group + size)
                faded = span(upper_group, upper_group + size, o)
                if b + 1 == bits:
                    last_group = chip - lax.rem(chip, chips_x // 2)
                    until_end = span(row_start, last_group + chips_x // 2, o)
                other = arrived(b, i)
                above = above + to_row * other
                if b + 1 < bits:
                    column = column * jnp.where(upper, 1.0, faded) + other * jnp.where(
                        upper, faded, 1.0
                    )
                    publish(b + 1, i, column)
                    yield
            before = jnp.zeros((DIM, DIM), F32)
            for b in range(1, bits_x + 1):
                size = 2 ** (b - 1)
                upper = is_upper(b)
                group = chip - lax.rem(chip, size)
                to_chip = jnp.where(upper, span(group, chip, o), 0.0)
                if b < bits_x:
                    publish(b, i, value)
                    publish(b, i, above, 1)
                    yield
                    other = arrived(b, i)
                    above = above + arrived(b, i, 1)
                    before = before + to_chip * other
                    upper_group = jnp.where(upper, group, group + size)
                    faded = span(upper_group, upper_group + size, o)
                    value = value * jnp.where(upper, 1.0, faded) + other * jnp.where(
                        upper, faded, 1.0
                    )
                else:
                    publish(b, i, jnp.where(upper, above, until_end * above + value))
                    yield
                    until_chip = span(row_start, chip, o)
                    before = before + until_chip * above
                    other = arrived(b, i)
                    before = before + jnp.where(upper, to_chip, until_chip) * other
            finish_head(i, before)
            yield

        routes = [straight(i) if i % 2 == 0 else crossed(i) for i in range(half)]

        def advance():
            for route in routes:
                next(route)

        def begin():
            for copy in first[:half]:
                copy.wait_recv()
            advance()

        def receive_rest():
            for copy in first[half:]:
                copy.wait_recv()
            for i in range(half):
                copies["pre", i].wait_recv()

        def finish():
            for copy in pending:
                copy.wait_send()

        def result(h):
            outside = pre[h]
            level = jnp.exp(levels[partners[0], pl.ds(h, 1), :])
            return jnp.where(is_upper(0), outside * level + recv[h], outside)

        return post, [begin] + [advance] * (bits - 1), result, receive_rest, finish

    other_first = [lax.rem(own + half + r, heads) for r in range(heads)]
    own_first = [lax.rem(own + r, heads) for r in range(heads)]

    def spot_columns(h):
        return pl.ds(pl.multiple_of(h * DIM, DIM), DIM)

    post, stages, start_state, receive_rest, finish_forward = exchange(
        False, f_send, f_recv, f_tsend, f_trecv, f_pre,
        fs_sem, fr_sem, fts_sem, ftr_sem, fps_sem, fpr_sem,
    )

    load_k.wait()
    load_v.wait()
    for r, h in enumerate(other_first):
        row = cum_rows[pl.ds(h, 1), :]
        turned = k[:, spot_columns(h)].T.astype(F32)
        weighted_keys = (turned * jnp.exp(row[:, tokens - 1 :] - row)).astype(BF16)
        post(r, h, dot(weighted_keys, v[:, spot_columns(h)], (1, 0)))

    load_q.wait()

    def forward(h, i):
        rows = slice(i * TILE, (i + 1) * TILE)
        total_rows = None
        for j in range(i + 1):
            sources = slice(j * TILE, (j + 1) * TILE)
            scores = dot(q[rows, columns(h)], k[sources, columns(h)], (1, 1))
            spread = cum[rows, h : h + 1] - cum_rows[h : h + 1, sources]
            if i == j:
                spread = jnp.where(diagonal, spread, -1e30)
            decays = jnp.exp(spread)
            dec[h, rows, sources] = decays
            mixing = (scores * decays).astype(BF16)
            mix[h, sources, rows] = mixing.T
            part = dot(mixing, v[sources, columns(h)], (1, 0))
            total_rows = part if total_rows is None else total_rows + part
        att[rows, columns(h)] = total_rows

    def weigh_queries():
        for h in range(heads):
            turned = q[:, columns(h)].T.astype(F32)
            wq[columns(h), :] = (turned * jnp.exp(cum_rows[h : h + 1, :])).astype(BF16)

    def units(work):
        return [functools.partial(work, h, i) for h in range(heads) for i in range(tiles)]

    def interleave(works, stages):
        for place, stage in enumerate(stages):
            for work in works[place] if place < len(works) else ():
                work()
            stage()

    def receive_levels():
        for copy in level_copies:
            copy.wait()

    def spread_factors():
        starting = jnp.exp(cum[...])
        ending = jnp.exp(cum[tokens - 1 : tokens, :] - cum[...])
        for h in range(heads):
            start_factor[h] = jnp.broadcast_to(starting[:, h : h + 1], (tokens, DIM))
            end_factor[h] = jnp.broadcast_to(ending[:, h : h + 1], (tokens, DIM))

    parts = units(forward)
    middle = len(parts) // 2
    interleave([[receive_levels], parts[:middle], [spread_factors] + parts[middle:]], stages)

    load_gain.wait()
    load_up.wait()
    for r, h in enumerate(own_first):
        if r == half:
            receive_rest()
        at = spot_columns(h)
        high, low = split(start_state(h))
        states[h] = jnp.concatenate([high, low], axis=1)
        queries = q[:, at]
        carried = dot(
            jnp.concatenate([queries, queries], axis=1), jnp.concatenate([high, low], axis=0), (1, 0)
        )
        value = att[:, at] + start_factor[h] * carried
        att[:, at] = value
        scaled = gain[:, at] * up[:, at].astype(F32)
        square, cross = value * value, scaled * value
        squares = square if r == 0 else squares + square
        crosses = cross if r == 0 else crosses + cross
    square_sum = jnp.sum(squares, axis=1, keepdims=True)
    cross_sum = jnp.sum(crosses, axis=1, keepdims=True)
    lane = lax.broadcasted_iota(jnp.int32, (tokens, DIM), 1)
    packed = jnp.where(lane == 0, square_sum, jnp.where(lane == 1, cross_sum, 0.0))
    z_send[...] = packed.T[:2]
    z_copies = []
    for d in range(1, head_n):
        copy = pltpu.make_async_remote_copy(
            src_ref=z_send, dst_ref=z_recv.at[d - 1],
            send_sem=zs_sem.at[d - 1], recv_sem=zr_sem.at[d - 1],
            device_id=(me, lax.rem(zed + d, head_n)), device_id_type=MESH,
        )
        copy.start()
        z_copies.append(copy)
    weigh_queries()
    finish_forward()
    sums = z_send[...]
    for d in range(1, head_n):
        z_copies[d - 1].wait_recv()
        sums = sums + z_recv[d - 1]
    inverse = lax.rsqrt(sums[0:1] / width + EPSILON)
    factor = inverse * inverse * inverse * sums[1:2] / width
    full = jnp.concatenate([inverse, factor, jnp.zeros((DIM - 2, tokens), F32)], axis=0).T
    inverse = jnp.broadcast_to(full[:, 0:1], (tokens, DIM))
    factor = jnp.broadcast_to(full[:, 1:2], (tokens, DIM))

    post, stages, end_state, receive_rest, finish_backward = exchange(
        True, b_send, b_recv, b_tsend, b_trecv, b_pre,
        bs_sem, br_sem, bts_sem, btr_sem, bps_sem, bpr_sem,
    )
    for r, h in enumerate(other_first):
        at = spot_columns(h)
        scaled = gain[:, at] * up[:, at].astype(F32)
        value = (inverse * scaled - att[:, at] * factor).astype(BF16)
        grad[:, at] = value
        post(r, h, dot(wq[at, :], value, (1, 0)))
    for copy in z_copies:
        copy.wait_send()

    def backward(h, i):
        rows = slice(i * TILE, (i + 1) * TILE)
        grads = grad[rows, columns(h)]
        query_sum = start_factor[h, rows] * dot(
            jnp.concatenate([grads, grads], axis=1), states[h], (1, 1)
        )
        for j in range(i + 1):
            sources = slice(j * TILE, (j + 1) * TILE)
            scores = dot(grads, v[sources, columns(h)], (1, 1))
            mixing = (scores * dec[h, rows, sources]).astype(BF16)
            query_sum = query_sum + dot(mixing, k[sources, columns(h)], (1, 0))
            key_part = dot(mixing, q[rows, columns(h)], (0, 0))
            value_part = dot(mix[h, sources, rows], grads, (1, 0))
            if i == j:
                dkp[sources, columns(h)] = key_part
                dvp[sources, columns(h)] = value_part
            else:
                dkp[sources, columns(h)] += key_part
                dvp[sources, columns(h)] += value_part
        dq[rows, columns(h)] = query_sum.astype(BF16)

    parts = units(backward)
    interleave([[], parts[:middle], parts[middle:]], stages)

    for r, h in enumerate(own_first):
        if r == half:
            receive_rest()
        at = spot_columns(h)
        high, low = split(end_state(h))
        ending = end_factor[h]
        keys, values = k[:, at], v[:, at]
        key_carried = dot(
            jnp.concatenate([values, values], axis=1), jnp.concatenate([high, low], axis=1), (1, 1)
        )
        dk[:, at] = (ending * key_carried + dkp[:, at]).astype(BF16)
        value_carried = dot(
            jnp.concatenate([keys, keys], axis=1), jnp.concatenate([high, low], axis=0), (1, 0)
        )
        dv[:, at] = (ending * value_carried + dvp[:, at]).astype(BF16)
    finish_backward()


def hand_over(*refs):
    count = (len(refs) - 1) // 2
    sem = refs[-1]
    copies = []
    for i in range(count):
        size = refs[i].shape[0] // COPIES
        for part in range(COPIES):
            rows = pl.ds(part * size, size)
            copy = pltpu.make_async_copy(
                refs[i].at[rows], refs[count + i].at[rows], sem.at[i * COPIES + part]
            )
            copy.start()
            copies.append(copy)
    for copy in copies:
        copy.wait()


def on_device(queries, keys, values, log_decay, gain, upstream):
    tokens, local = queries.shape
    heads = log_decay.shape[1]
    ctx_n, head_n = lax.axis_size("ctx"), lax.axis_size("head")
    slots = (ctx_n.bit_length() - 2) * heads
    half = heads // 2
    wide = (tokens, local)
    message = (heads, DIM, DIM)
    chip_message = (slots, DIM, DIM)
    states = [
        pltpu.VMEM(message, F32),
        pltpu.VMEM(message, F32),
        pltpu.VMEM(chip_message, F32),
        pltpu.VMEM(chip_message, F32),
        pltpu.VMEM((heads, DIM, DIM), F32),
    ]
    dma = pltpu.SemaphoreType.DMA
    state_sems = [
        dma((heads,)), dma((heads,)), dma((slots,)), dma((slots,)),
        dma((half,)), dma((half,)),
    ]
    in_vmem = pl.BlockSpec(memory_space=pltpu.VMEM)
    in_hbm = pl.BlockSpec(memory_space=pltpu.HBM)
    out = jax.ShapeDtypeStruct(wide, BF16)
    results = pl.pallas_call(
        functools.partial(kernel, ctx_n, head_n, local * head_n),
        out_shape=(pltpu.VMEM(wide, BF16),) * 3,
        in_specs=[in_hbm] * 6,
        out_specs=(in_vmem,) * 3,
        scratch_shapes=[
            pltpu.VMEM(wide, BF16),
            pltpu.VMEM(wide, BF16),
            pltpu.VMEM(wide, BF16),
            pltpu.VMEM((heads, tokens), F32),
            pltpu.VMEM((1, local), F32),
            pltpu.VMEM(wide, BF16),
            pltpu.VMEM((heads, tokens, tokens), BF16),
            pltpu.VMEM((heads, tokens, tokens), F32),
            pltpu.VMEM(wide, F32),
            pltpu.VMEM(wide, BF16),
            pltpu.VMEM((local, tokens), BF16),
            pltpu.VMEM((tokens, DIM), F32),
            pltpu.VMEM((8, tokens), F32),
            pltpu.VMEM(wide, F32),
            pltpu.VMEM(wide, F32),
            pltpu.VMEM((heads, tokens, DIM), F32),
            pltpu.VMEM((heads, tokens, DIM), F32),
            pltpu.VMEM((heads, DIM, 2 * DIM), BF16),
            *states,
            *states,
            pltpu.VMEM((2, tokens), F32),
            pltpu.VMEM((head_n - 1, 2, tokens), F32),
            pltpu.VMEM((ctx_n, 8, DIM), F32),
            dma((6,)),
            *state_sems,
            *state_sems,
            dma((head_n - 1,)),
            dma((head_n - 1,)),
            dma((ctx_n - 1,)),
            dma((ctx_n - 1,)),
        ],
        compiler_params=pltpu.CompilerParams(
            collective_id=0, has_side_effects=True, vmem_limit_bytes=60 * 2**20
        ),
        cost_estimate=pl.CostEstimate(
            flops=16 * heads * tokens * tokens * DIM,
            bytes_accessed=14 * tokens * local,
            transcendentals=heads * tokens * tokens,
        ),
    )(queries, keys, values, log_decay.T, gain.reshape(1, -1), upstream)
    return pl.pallas_call(
        hand_over,
        out_shape=(out, out, out),
        in_specs=[in_vmem] * 3,
        out_specs=(in_hbm,) * 3,
        scratch_shapes=[dma((3 * COPIES,))],
        compiler_params=pltpu.CompilerParams(vmem_limit_bytes=8 * 2**20),
    )(*results)


def solution(mesh):
    wide = P("ctx", "head")
    return jax.shard_map(
        on_device,
        mesh=mesh,
        in_specs=(wide, wide, wide, wide, P("head"), wide),
        out_specs=(wide, wide, wide),
        check_vma=False,
    )
```

```python
import functools

import jax
import jax.numpy as jnp
from jax import lax
from jax.experimental import pallas as pl
from jax.experimental.pallas import tpu as pltpu
from jax.sharding import PartitionSpec as P

DIM = 128
TILE = 256
COPIES = 4
PARTS = 2
EPSILON = 1e-06
MESH = pl.DeviceIdType.MESH
F32 = jnp.float32
BF16 = jnp.bfloat16


def dot(a, b, dims):
    return lax.dot_general(a, b, ((dims[:1], dims[1:]), ((), ())), preferred_element_type=F32)


def split(x):
    high = x.astype(BF16)
    return high, (x - high.astype(F32)).astype(BF16)


def kernel(
    ctx_n, head_n, width,
    q_hbm, k_hbm, v_hbm, ld_hbm, gain_hbm, up_hbm,
    dq, dk, dv,
    q, k, v, ld, gain, up,
    mix, dec, att, grad, wq, cum, cum_rows, dkp, dvp, start_factor, end_factor, states, qt, dkt,
    f_send, f_recv, f_tsend, f_trecv, f_pre,
    b_send, b_recv, b_tsend, b_trecv, b_pre,
    z_send, z_recv, levels,
    in_sem,
    fs_sem, fr_sem, fts_sem, ftr_sem, fps_sem, fpr_sem,
    bs_sem, br_sem, bts_sem, btr_sem, bps_sem, bpr_sem,
    zs_sem, zr_sem, ls_sem, lr_sem,
):
    tokens = q.shape[0]
    heads = q.shape[1] // DIM
    half = heads // 2
    bits = ctx_n.bit_length() - 1
    bits_x = (bits - 1) // 2
    chips_x = 2**bits_x
    tiles = tokens // TILE
    me = lax.axis_index("ctx")
    zed = lax.axis_index("head")
    core = lax.rem(me, 2)
    own = core * half
    bit_values = [lax.rem(me // (2**b), 2) for b in range(bits)]
    partners = [me + (2**b) * (1 - 2 * bit_values[b]) for b in range(bits)]

    def load(number, src, dst, parts):
        size = src.shape[0] // parts
        copies = []
        for part in range(parts):
            rows = pl.ds(part * size, size)
            copy = pltpu.make_async_copy(
                src.at[rows], dst.at[rows], in_sem.at[number * COPIES + part]
            )
            copy.start()
            copies.append(copy)
        return copies

    def wait(copies):
        for copy in copies:
            copy.wait()

    load_ld = load(0, ld_hbm, ld, 1)
    load_k = load(1, k_hbm, k, COPIES)
    load_v = load(2, v_hbm, v, COPIES)
    load_q = load(3, q_hbm, q, COPIES)
    load_gain = load(4, gain_hbm, gain, 1)
    load_up = load(5, up_hbm, up, COPIES)

    barrier = pltpu.get_barrier_semaphore()
    for d in range(1, ctx_n):
        pl.semaphore_signal(
            barrier, inc=1, device_id=(lax.rem(me + d, ctx_n), zed), device_id_type=MESH
        )
    for d in range(1, head_n):
        pl.semaphore_signal(
            barrier, inc=1, device_id=(me, lax.rem(zed + d, head_n)), device_id_type=MESH
        )

    row_id = lax.broadcasted_iota(jnp.int32, (tokens, tokens), 0)
    col_id = lax.broadcasted_iota(jnp.int32, (tokens, tokens), 1)
    until = jnp.where(row_id <= col_id, 1.0, 0.0).astype(BF16)
    wait(load_ld)
    steps = jnp.pad(ld[...], ((0, 8 - heads), (0, 0)))
    top = steps.astype(BF16).astype(F32)
    rest = (steps - top).astype(BF16).astype(F32)
    parts = jnp.concatenate([top, rest, steps - top - rest, jnp.zeros_like(steps)], axis=0)
    sums = dot(parts.astype(BF16), until, (1, 0))
    rows_cum = sums[:8] + (sums[8:16] + sums[16:24])
    cum_rows[...] = rows_cum
    cum[...] = jnp.concatenate([rows_cum, jnp.zeros((DIM - 8, tokens), F32)], axis=0).T

    levels[me] = jnp.broadcast_to(rows_cum[:, tokens - 1 :], (8, DIM))
    pl.semaphore_wait(barrier, ctx_n + head_n - 2)
    level_copies = []
    for d in range(1, ctx_n):
        copy = pltpu.make_async_remote_copy(
            src_ref=levels.at[me], dst_ref=levels.at[me],
            send_sem=ls_sem.at[d - 1], recv_sem=lr_sem.at[d - 1],
            device_id=(lax.rem(me + d, ctx_n), zed), device_id_type=MESH,
        )
        copy.start()
        level_copies.append(copy)

    def columns(h):
        return slice(h * DIM, (h + 1) * DIM)

    diagonal = lax.broadcasted_iota(jnp.int32, (TILE, TILE), 0) >= lax.broadcasted_iota(
        jnp.int32, (TILE, TILE), 1
    )

    def exchange(rev, send, recv, tsend, trecv, pre, ss, rs, tss, trs, pss, prs):
        pending = []
        spot = ctx_n - 1 - me if rev else me
        chip = spot // 2
        row_start = chip - lax.rem(chip, chips_x)

        def remote(src, dst, s_sem, r_sem, b):
            copy = pltpu.make_async_remote_copy(
                src_ref=src, dst_ref=dst, send_sem=s_sem, recv_sem=r_sem,
                device_id=(partners[b], zed), device_id_type=MESH,
            )
            copy.start()
            pending.append(copy)
            return copy

        def span(first, last, o):
            total_level = jnp.zeros((1, DIM), F32)
            for j in range(ctx_n):
                place = (ctx_n - 1 - j if rev else j) // 2
                inside = jnp.logical_and(first <= place, place < last)
                total_level = total_level + jnp.where(inside, levels[j, pl.ds(o, 1), :], 0.0)
            return jnp.exp(total_level)

        def is_upper(b):
            return lax.rem(spot // (2**b), 2) == 1

        first = []

        def post(r, h, value):
            send[h] = value
            first.append(remote(send.at[h], recv.at[h], ss.at[r], rs.at[r], 0))

        def slot_of(b, i, second):
            head, part = i
            return (((b - 1) * half + head) * PARTS + part) * 2 + second

        copies = {}

        def publish(b, i, value, second=0):
            slot = slot_of(b, i, second)
            tsend[slot] = value
            copies[b, i, second] = remote(
                tsend.at[slot], trecv.at[slot], tss.at[slot], trs.at[slot], b
            )

        def arrived(b, i, second=0):
            copies[b, i, second].wait_recv()
            return trecv[slot_of(b, i, second)]

        def rows_of(i):
            return pl.ds(i[1] * (DIM // PARTS), DIM // PARTS)

        def finish_head(i, value):
            at = (own + i[0], rows_of(i))
            number = i[0] * PARTS + i[1]
            pre[at] = value
            copies["pre", i] = remote(pre.at[at], pre.at[at], pss.at[number], prs.at[number], 0)

        def pair(i):
            o, rows = own + i[0], rows_of(i)
            first_level = jnp.exp(levels[me, pl.ds(o, 1), :])
            other_level = jnp.exp(levels[partners[0], pl.ds(o, 1), :])
            upper = is_upper(0)
            return send[o, rows] * jnp.where(upper, 1.0, other_level) + recv[o, rows] * jnp.where(
                upper, first_level, 1.0
            )

        def straight(i):
            o = own + i[0]
            value = pair(i)
            publish(1, i, value)
            yield
            before = jnp.zeros((DIM // PARTS, DIM), F32)
            for b in range(1, bits):
                size = 2 ** (b - 1)
                upper = is_upper(b)
                group = chip - lax.rem(chip, size)
                to_chip = jnp.where(upper, span(group, chip, o), 0.0)
                upper_group = jnp.where(upper, group, group + size)
                faded = span(upper_group, upper_group + size, o)
                other = arrived(b, i)
                before = before + to_chip * other
                if b + 1 < bits:
                    value = value * jnp.where(upper, 1.0, faded) + other * jnp.where(
                        upper, faded, 1.0
                    )
                    publish(b + 1, i, value)
                    yield
            finish_head(i, before)
            yield

        def crossed(i):
            o = own + i[0]
            value = pair(i)
            column = value * span(chip + 1, row_start + chips_x, o)
            publish(bits_x + 1, i, column)
            yield
            above = jnp.zeros((DIM // PARTS, DIM), F32)
            for b in range(bits_x + 1, bits):
                size = 2 ** (b - 1)
                upper = is_upper(b)
                group = chip - lax.rem(chip, size)
                to_row = jnp.where(upper, span(group, row_start, o), 0.0)
                upper_group = jnp.where(upper, group, group + size)
                faded = span(upper_group, upper_group + size, o)
                if b + 1 == bits:
                    last_group = chip - lax.rem(chip, chips_x // 2)
                    until_end = span(row_start, last_group + chips_x // 2, o)
                other = arrived(b, i)
                above = above + to_row * other
                if b + 1 < bits:
                    column = column * jnp.where(upper, 1.0, faded) + other * jnp.where(
                        upper, faded, 1.0
                    )
                    publish(b + 1, i, column)
                    yield
            before = jnp.zeros((DIM // PARTS, DIM), F32)
            for b in range(1, bits_x + 1):
                size = 2 ** (b - 1)
                upper = is_upper(b)
                group = chip - lax.rem(chip, size)
                to_chip = jnp.where(upper, span(group, chip, o), 0.0)
                if b < bits_x:
                    publish(b, i, value)
                    publish(b, i, above, 1)
                    yield
                    other = arrived(b, i)
                    above = above + arrived(b, i, 1)
                    before = before + to_chip * other
                    upper_group = jnp.where(upper, group, group + size)
                    faded = span(upper_group, upper_group + size, o)
                    value = value * jnp.where(upper, 1.0, faded) + other * jnp.where(
                        upper, faded, 1.0
                    )
                else:
                    publish(b, i, jnp.where(upper, above, until_end * above + value))
                    yield
                    until_chip = span(row_start, chip, o)
                    before = before + until_chip * above
                    other = arrived(b, i)
                    before = before + jnp.where(upper, to_chip, until_chip) * other
            finish_head(i, before)
            yield

        routes = [
            [(crossed if i % 2 else straight)((i, part)) for i in range(half)]
            for part in range(PARTS)
        ]

        def advance(part):
            for route in routes[part]:
                next(route)

        def begin():
            for copy in first[:half]:
                copy.wait_recv()
            for part in range(PARTS):
                advance(part)

        def receive_rest():
            for copy in first[half:]:
                copy.wait_recv()
            for i in range(half):
                for part in range(PARTS):
                    copies["pre", (i, part)].wait_recv()

        def finish():
            for copy in pending:
                copy.wait_send()

        def result(h):
            outside = pre[h]
            level = jnp.exp(levels[partners[0], pl.ds(h, 1), :])
            return jnp.where(is_upper(0), outside * level + recv[h], outside)

        steps = [functools.partial(advance, part) for part in range(PARTS)] * (bits - 1)
        return post, [begin] + steps, result, receive_rest, finish

    other_first = [lax.rem(own + half + r, heads) for r in range(heads)]
    own_first = [lax.rem(own + r, heads) for r in range(heads)]

    def spot_columns(h):
        return pl.ds(pl.multiple_of(h * DIM, DIM), DIM)

    post, stages, start_state, receive_rest, finish_forward = exchange(
        False, f_send, f_recv, f_tsend, f_trecv, f_pre,
        fs_sem, fr_sem, fts_sem, ftr_sem, fps_sem, fpr_sem,
    )

    wait(load_k)
    wait(load_v)
    for r, h in enumerate(other_first):
        row = cum_rows[pl.ds(h, 1), :]
        turned = k[:, spot_columns(h)].T.astype(F32)
        weighted_keys = (turned * jnp.exp(row[:, tokens - 1 :] - row)).astype(BF16)
        post(r, h, dot(weighted_keys, v[:, spot_columns(h)], (1, 0)))

    wait(load_q)

    def forward(h, i):
        rows = slice(i * TILE, (i + 1) * TILE)
        total_rows = None
        for j in range(i + 1):
            sources = slice(j * TILE, (j + 1) * TILE)
            scores = dot(q[rows, columns(h)], k[sources, columns(h)], (1, 1))
            spread = cum[rows, h : h + 1] - cum_rows[h : h + 1, sources]
            if i == j:
                spread = jnp.where(diagonal, spread, -1e30)
            decays = jnp.exp(spread)
            dec[h, rows, sources] = decays
            mixing = (scores * decays).astype(BF16)
            mix[h, sources, rows] = mixing.T
            part = dot(mixing, v[sources, columns(h)], (1, 0))
            total_rows = part if total_rows is None else total_rows + part
        att[rows, columns(h)] = total_rows

    def weigh_queries():
        for h in range(heads):
            turned = q[:, columns(h)].T.astype(F32)
            qt[columns(h), :] = turned.astype(BF16)
            wq[columns(h), :] = (turned * jnp.exp(cum_rows[h : h + 1, :])).astype(BF16)

    def units(work):
        return [functools.partial(work, h, i) for h in range(heads) for i in range(tiles)]

    def interleave(works, stages):
        for place, stage in enumerate(stages):
            for work in works[place] if place < len(works) else ():
                work()
            stage()

    def receive_levels():
        for copy in level_copies:
            copy.wait()

    def spread_factors():
        starting = jnp.exp(cum[...])
        ending = jnp.exp(cum[tokens - 1 : tokens, :] - cum[...])
        for h in range(heads):
            start_factor[h] = jnp.broadcast_to(starting[:, h : h + 1], (tokens, DIM))
            end_factor[h] = jnp.broadcast_to(ending[:, h : h + 1], (tokens, DIM))

    parts = units(forward)
    shares = [parts[tiles * h : tiles * (h + 1)] for h in range(heads)]
    interleave([[receive_levels]] + shares[:-1] + [[spread_factors] + shares[-1]], stages)

    wait(load_gain)
    wait(load_up)
    for r, h in enumerate(own_first):
        if r == half:
            receive_rest()
        at = spot_columns(h)
        high, low = split(start_state(h))
        states[h] = jnp.concatenate([high, low], axis=1)
        queries = q[:, at]
        carried = dot(
            jnp.concatenate([queries, queries], axis=1), jnp.concatenate([high, low], axis=0), (1, 0)
        )
        value = att[:, at] + start_factor[h] * carried
        att[:, at] = value
        scaled = gain[:, at] * up[:, at].astype(F32)
        square, cross = value * value, scaled * value
        squares = square if r == 0 else squares + square
        crosses = cross if r == 0 else crosses + cross
    ones = jnp.ones((16, 2 * DIM), BF16)
    for place, addends in enumerate((squares, crosses)):
        high, low = split(addends)
        added = dot(ones, jnp.concatenate([high, low], axis=1), (1, 1))
        z_send[place : place + 1] = added[:1]
    z_copies = []
    for d in range(1, head_n):
        copy = pltpu.make_async_remote_copy(
            src_ref=z_send, dst_ref=z_recv.at[d - 1],
            send_sem=zs_sem.at[d - 1], recv_sem=zr_sem.at[d - 1],
            device_id=(me, lax.rem(zed + d, head_n)), device_id_type=MESH,
        )
        copy.start()
        z_copies.append(copy)
    weigh_queries()
    finish_forward()
    sums = z_send[...]
    for d in range(1, head_n):
        z_copies[d - 1].wait_recv()
        sums = sums + z_recv[d - 1]
    inverse = lax.rsqrt(sums[0:1] / width + EPSILON)
    factor = inverse * inverse * inverse * sums[1:2] / width
    full = jnp.concatenate([inverse, factor, jnp.zeros((DIM - 2, tokens), F32)], axis=0).T
    inverse = jnp.broadcast_to(full[:, 0:1], (tokens, DIM))
    factor = jnp.broadcast_to(full[:, 1:2], (tokens, DIM))

    post, stages, end_state, receive_rest, finish_backward = exchange(
        True, b_send, b_recv, b_tsend, b_trecv, b_pre,
        bs_sem, br_sem, bts_sem, btr_sem, bps_sem, bpr_sem,
    )
    for r, h in enumerate(other_first):
        at = spot_columns(h)
        scaled = gain[:, at] * up[:, at].astype(F32)
        value = (inverse * scaled - att[:, at] * factor).astype(BF16)
        grad[:, at] = value
        post(r, h, dot(wq[at, :], value, (1, 0)))
    for copy in z_copies:
        copy.wait_send()

    def backward(h, i):
        rows = slice(i * TILE, (i + 1) * TILE)
        grads = grad[rows, columns(h)]
        query_sum = start_factor[h, rows] * dot(
            jnp.concatenate([grads, grads], axis=1), states[h], (1, 1)
        )
        for j in range(i + 1):
            sources = slice(j * TILE, (j + 1) * TILE)
            scores = dot(grads, v[sources, columns(h)], (1, 1))
            mixing = (scores * dec[h, rows, sources]).astype(BF16)
            query_sum = query_sum + dot(mixing, k[sources, columns(h)], (1, 0))
            key_part = dot(qt[columns(h), rows], mixing, (1, 0))
            value_part = dot(mix[h, sources, rows], grads, (1, 0))
            if i == j:
                dkt[columns(h), sources] = key_part
                dvp[sources, columns(h)] = value_part
            else:
                dkt[columns(h), sources] += key_part
                dvp[sources, columns(h)] += value_part
        dq[rows, columns(h)] = query_sum.astype(BF16)
        if i == tiles - 1:
            dkp[:, columns(h)] = dkt[columns(h), :].T

    parts = units(backward)
    shares = [parts[tiles * h : tiles * (h + 1)] for h in range(heads)]
    interleave([[]] + shares, stages)

    for r, h in enumerate(own_first):
        if r == half:
            receive_rest()
        at = spot_columns(h)
        high, low = split(end_state(h))
        ending = end_factor[h]
        keys, values = k[:, at], v[:, at]
        key_carried = dot(
            jnp.concatenate([values, values], axis=1), jnp.concatenate([high, low], axis=1), (1, 1)
        )
        dk[:, at] = (ending * key_carried + dkp[:, at]).astype(BF16)
        value_carried = dot(
            jnp.concatenate([keys, keys], axis=1), jnp.concatenate([high, low], axis=0), (1, 0)
        )
        dv[:, at] = (ending * value_carried + dvp[:, at]).astype(BF16)
    finish_backward()


def hand_over(*refs):
    count = (len(refs) - 1) // 2
    sem = refs[-1]
    copies = []
    for i in range(count):
        size = refs[i].shape[0] // COPIES
        for part in range(COPIES):
            rows = pl.ds(part * size, size)
            copy = pltpu.make_async_copy(
                refs[i].at[rows], refs[count + i].at[rows], sem.at[i * COPIES + part]
            )
            copy.start()
            copies.append(copy)
    for copy in copies:
        copy.wait()


def on_device(queries, keys, values, log_decay, gain, upstream):
    tokens, local = queries.shape
    heads = log_decay.shape[1]
    ctx_n, head_n = lax.axis_size("ctx"), lax.axis_size("head")
    slots = (ctx_n.bit_length() - 2) * heads * PARTS
    half = heads // 2
    wide = (tokens, local)
    message = (heads, DIM, DIM)
    chip_message = (slots, DIM // PARTS, DIM)
    states = [
        pltpu.VMEM(message, F32),
        pltpu.VMEM(message, F32),
        pltpu.VMEM(chip_message, F32),
        pltpu.VMEM(chip_message, F32),
        pltpu.VMEM((heads, DIM, DIM), F32),
    ]
    dma = pltpu.SemaphoreType.DMA
    state_sems = [
        dma((heads,)), dma((heads,)), dma((slots,)), dma((slots,)),
        dma((half * PARTS,)), dma((half * PARTS,)),
    ]
    in_vmem = pl.BlockSpec(memory_space=pltpu.VMEM)
    in_hbm = pl.BlockSpec(memory_space=pltpu.HBM)
    out = jax.ShapeDtypeStruct(wide, BF16)
    results = pl.pallas_call(
        functools.partial(kernel, ctx_n, head_n, local * head_n),
        out_shape=(pltpu.VMEM(wide, BF16),) * 3,
        in_specs=[in_hbm] * 6,
        out_specs=(in_vmem,) * 3,
        scratch_shapes=[
            pltpu.VMEM(wide, BF16),
            pltpu.VMEM(wide, BF16),
            pltpu.VMEM(wide, BF16),
            pltpu.VMEM((heads, tokens), F32),
            pltpu.VMEM((1, local), F32),
            pltpu.VMEM(wide, BF16),
            pltpu.VMEM((heads, tokens, tokens), BF16),
            pltpu.VMEM((heads, tokens, tokens), F32),
            pltpu.VMEM(wide, F32),
            pltpu.VMEM(wide, BF16),
            pltpu.VMEM((local, tokens), BF16),
            pltpu.VMEM((tokens, DIM), F32),
            pltpu.VMEM((8, tokens), F32),
            pltpu.VMEM(wide, F32),
            pltpu.VMEM(wide, F32),
            pltpu.VMEM((heads, tokens, DIM), F32),
            pltpu.VMEM((heads, tokens, DIM), F32),
            pltpu.VMEM((heads, DIM, 2 * DIM), BF16),
            pltpu.VMEM((local, tokens), BF16),
            pltpu.VMEM((local, tokens), F32),
            *states,
            *states,
            pltpu.VMEM((2, tokens), F32),
            pltpu.VMEM((head_n - 1, 2, tokens), F32),
            pltpu.VMEM((ctx_n, 8, DIM), F32),
            dma((6 * COPIES,)),
            *state_sems,
            *state_sems,
            dma((head_n - 1,)),
            dma((head_n - 1,)),
            dma((ctx_n - 1,)),
            dma((ctx_n - 1,)),
        ],
        compiler_params=pltpu.CompilerParams(
            collective_id=0, has_side_effects=True, vmem_limit_bytes=60 * 2**20
        ),
        cost_estimate=pl.CostEstimate(
            flops=16 * heads * tokens * tokens * DIM,
            bytes_accessed=14 * tokens * local,
            transcendentals=heads * tokens * tokens,
        ),
    )(queries, keys, values, log_decay.T, gain.reshape(1, -1), upstream)
    return pl.pallas_call(
        hand_over,
        out_shape=(out, out, out),
        in_specs=[in_vmem] * 3,
        out_specs=(in_hbm,) * 3,
        scratch_shapes=[dma((3 * COPIES,))],
        compiler_params=pltpu.CompilerParams(vmem_limit_bytes=8 * 2**20),
    )(*results)


def solution(mesh):
    wide = P("ctx", "head")
    return jax.shard_map(
        on_device,
        mesh=mesh,
        in_specs=(wide, wide, wide, wide, P("head"), wide),
        out_specs=(wide, wide, wide),
        check_vma=False,
    )
```

```python
import functools

import jax
import jax.numpy as jnp
from jax import lax
from jax.experimental import pallas as pl
from jax.experimental.pallas import tpu as pltpu
from jax.sharding import PartitionSpec as P

DIM = 128
TILE = 256
COPIES = 4
PARTS = 1
EPSILON = 1e-06
MESH = pl.DeviceIdType.MESH
F32 = jnp.float32
BF16 = jnp.bfloat16


def dot(a, b, dims):
    return lax.dot_general(a, b, ((dims[:1], dims[1:]), ((), ())), preferred_element_type=F32)


def split(x):
    high = x.astype(BF16)
    return high, (x - high.astype(F32)).astype(BF16)


def kernel(
    ctx_n, head_n, width,
    q_hbm, k_hbm, v_hbm, ld_hbm, gain_hbm, up_hbm,
    dq, dk, dv,
    q, k, v, ld, gain, up,
    mix, dec, att, grad, wq, cum, cum_rows, dkp, dvp, start_factor, end_factor, states, qt, dkt,
    f_send, f_recv, f_tsend, f_trecv, f_pre,
    b_send, b_recv, b_tsend, b_trecv, b_pre,
    z_send, z_recv, levels,
    in_sem,
    fs_sem, fr_sem, fts_sem, ftr_sem, fps_sem, fpr_sem,
    bs_sem, br_sem, bts_sem, btr_sem, bps_sem, bpr_sem,
    zs_sem, zr_sem, ls_sem, lr_sem,
):
    tokens = q.shape[0]
    heads = q.shape[1] // DIM
    half = heads // 2
    bits = ctx_n.bit_length() - 1
    bits_x = (bits - 1) // 2
    chips_x = 2**bits_x
    tiles = tokens // TILE
    me = lax.axis_index("ctx")
    zed = lax.axis_index("head")
    core = lax.rem(me, 2)
    own = core * half
    bit_values = [lax.rem(me // (2**b), 2) for b in range(bits)]
    partners = [me + (2**b) * (1 - 2 * bit_values[b]) for b in range(bits)]

    def load(number, src, dst, parts):
        size = src.shape[0] // parts
        copies = []
        for part in range(parts):
            rows = pl.ds(part * size, size)
            copy = pltpu.make_async_copy(
                src.at[rows], dst.at[rows], in_sem.at[number * COPIES + part]
            )
            copy.start()
            copies.append(copy)
        return copies

    def wait(copies):
        for copy in copies:
            copy.wait()

    load_ld = load(0, ld_hbm, ld, 1)
    load_k = load(1, k_hbm, k, 2)
    load_v = load(2, v_hbm, v, 2)

    barrier = pltpu.get_barrier_semaphore()
    for d in range(1, ctx_n):
        pl.semaphore_signal(
            barrier, inc=1, device_id=(lax.rem(me + d, ctx_n), zed), device_id_type=MESH
        )
    for d in range(1, head_n):
        pl.semaphore_signal(
            barrier, inc=1, device_id=(me, lax.rem(zed + d, head_n)), device_id_type=MESH
        )

    load_q = load(3, q_hbm, q, 1)
    load_gain = load(4, gain_hbm, gain, 1)
    load_up = load(5, up_hbm, up, 1)

    row_id = lax.broadcasted_iota(jnp.int32, (tokens, tokens), 0)
    col_id = lax.broadcasted_iota(jnp.int32, (tokens, tokens), 1)
    until = jnp.where(row_id <= col_id, 1.0, 0.0).astype(BF16)
    wait(load_ld)
    steps = jnp.pad(ld[...], ((0, 8 - heads), (0, 0)))
    top = steps.astype(BF16).astype(F32)
    rest = (steps - top).astype(BF16).astype(F32)
    parts = jnp.concatenate([top, rest, steps - top - rest, jnp.zeros_like(steps)], axis=0)
    sums = dot(parts.astype(BF16), until, (1, 0))
    rows_cum = sums[:8] + (sums[8:16] + sums[16:24])
    cum_rows[...] = rows_cum
    cum[...] = jnp.concatenate([rows_cum, jnp.zeros((DIM - 8, tokens), F32)], axis=0).T

    levels[me] = jnp.broadcast_to(rows_cum[:, tokens - 1 :], (8, DIM))
    pl.semaphore_wait(barrier, ctx_n + head_n - 2)
    level_copies = []
    for d in range(1, ctx_n):
        copy = pltpu.make_async_remote_copy(
            src_ref=levels.at[me], dst_ref=levels.at[me],
            send_sem=ls_sem.at[d - 1], recv_sem=lr_sem.at[d - 1],
            device_id=(lax.rem(me + d, ctx_n), zed), device_id_type=MESH,
        )
        copy.start()
        level_copies.append(copy)

    def columns(h):
        return slice(h * DIM, (h + 1) * DIM)

    diagonal = lax.broadcasted_iota(jnp.int32, (TILE, TILE), 0) >= lax.broadcasted_iota(
        jnp.int32, (TILE, TILE), 1
    )

    def exchange(rev, send, recv, tsend, trecv, pre, ss, rs, tss, trs, pss, prs):
        pending = []
        spot = ctx_n - 1 - me if rev else me
        chip = spot // 2
        row_start = chip - lax.rem(chip, chips_x)

        def remote(src, dst, s_sem, r_sem, b):
            copy = pltpu.make_async_remote_copy(
                src_ref=src, dst_ref=dst, send_sem=s_sem, recv_sem=r_sem,
                device_id=(partners[b], zed), device_id_type=MESH,
            )
            copy.start()
            pending.append(copy)
            return copy

        def span(first, last, o):
            total_level = jnp.zeros((1, DIM), F32)
            for j in range(ctx_n):
                place = (ctx_n - 1 - j if rev else j) // 2
                inside = jnp.logical_and(first <= place, place < last)
                total_level = total_level + jnp.where(inside, levels[j, pl.ds(o, 1), :], 0.0)
            return jnp.exp(total_level)

        def is_upper(b):
            return lax.rem(spot // (2**b), 2) == 1

        first = []

        def post(r, h, value):
            send[h] = value
            first.append(remote(send.at[h], recv.at[h], ss.at[r], rs.at[r], 0))

        def slot_of(b, i, second):
            head, part = i
            return (((b - 1) * half + head) * PARTS + part) * 2 + second

        copies = {}

        def publish(b, i, value, second=0):
            slot = slot_of(b, i, second)
            tsend[slot] = value
            copies[b, i, second] = remote(
                tsend.at[slot], trecv.at[slot], tss.at[slot], trs.at[slot], b
            )

        def arrived(b, i, second=0):
            copies[b, i, second].wait_recv()
            return trecv[slot_of(b, i, second)]

        def rows_of(i):
            return pl.ds(i[1] * (DIM // PARTS), DIM // PARTS)

        def finish_head(i, value):
            at = (own + i[0], rows_of(i))
            number = i[0] * PARTS + i[1]
            pre[at] = value
            copies["pre", i] = remote(pre.at[at], pre.at[at], pss.at[number], prs.at[number], 0)

        def pair(i):
            o, rows = own + i[0], rows_of(i)
            first_level = jnp.exp(levels[me, pl.ds(o, 1), :])
            other_level = jnp.exp(levels[partners[0], pl.ds(o, 1), :])
            upper = is_upper(0)
            return send[o, rows] * jnp.where(upper, 1.0, other_level) + recv[o, rows] * jnp.where(
                upper, first_level, 1.0
            )

        def straight(i):
            o = own + i[0]
            value = pair(i)
            publish(1, i, value)
            yield
            before = jnp.zeros((DIM // PARTS, DIM), F32)
            for b in range(1, bits):
                size = 2 ** (b - 1)
                upper = is_upper(b)
                group = chip - lax.rem(chip, size)
                to_chip = jnp.where(upper, span(group, chip, o), 0.0)
                upper_group = jnp.where(upper, group, group + size)
                faded = span(upper_group, upper_group + size, o)
                other = arrived(b, i)
                before = before + to_chip * other
                if b + 1 < bits:
                    value = value * jnp.where(upper, 1.0, faded) + other * jnp.where(
                        upper, faded, 1.0
                    )
                    publish(b + 1, i, value)
                    yield
            finish_head(i, before)
            yield

        def crossed(i):
            o = own + i[0]
            value = pair(i)
            column = value * span(chip + 1, row_start + chips_x, o)
            publish(bits_x + 1, i, column)
            yield
            above = jnp.zeros((DIM // PARTS, DIM), F32)
            for b in range(bits_x + 1, bits):
                size = 2 ** (b - 1)
                upper = is_upper(b)
                group = chip - lax.rem(chip, size)
                to_row = jnp.where(upper, span(group, row_start, o), 0.0)
                upper_group = jnp.where(upper, group, group + size)
                faded = span(upper_group, upper_group + size, o)
                if b + 1 == bits:
                    last_group = chip - lax.rem(chip, chips_x // 2)
                    until_end = span(row_start, last_group + chips_x // 2, o)
                other = arrived(b, i)
                above = above + to_row * other
                if b + 1 < bits:
                    column = column * jnp.where(upper, 1.0, faded) + other * jnp.where(
                        upper, faded, 1.0
                    )
                    publish(b + 1, i, column)
                    yield
            before = jnp.zeros((DIM // PARTS, DIM), F32)
            for b in range(1, bits_x + 1):
                size = 2 ** (b - 1)
                upper = is_upper(b)
                group = chip - lax.rem(chip, size)
                to_chip = jnp.where(upper, span(group, chip, o), 0.0)
                if b < bits_x:
                    publish(b, i, value)
                    publish(b, i, above, 1)
                    yield
                    other = arrived(b, i)
                    above = above + arrived(b, i, 1)
                    before = before + to_chip * other
                    upper_group = jnp.where(upper, group, group + size)
                    faded = span(upper_group, upper_group + size, o)
                    value = value * jnp.where(upper, 1.0, faded) + other * jnp.where(
                        upper, faded, 1.0
                    )
                else:
                    publish(b, i, jnp.where(upper, above, until_end * above + value))
                    yield
                    until_chip = span(row_start, chip, o)
                    before = before + until_chip * above
                    other = arrived(b, i)
                    before = before + jnp.where(upper, to_chip, until_chip) * other
            finish_head(i, before)
            yield

        routes = [
            [(crossed if i % 2 else straight)((i, part)) for i in range(half)]
            for part in range(PARTS)
        ]

        def advance(part):
            for route in routes[part]:
                next(route)

        def begin():
            for copy in first[:half]:
                copy.wait_recv()
            for part in range(PARTS):
                advance(part)

        def receive_rest():
            for copy in first[half:]:
                copy.wait_recv()
            for i in range(half):
                for part in range(PARTS):
                    copies["pre", (i, part)].wait_recv()

        def finish():
            for copy in pending:
                copy.wait_send()

        def result(h):
            outside = pre[h]
            level = jnp.exp(levels[partners[0], pl.ds(h, 1), :])
            return jnp.where(is_upper(0), outside * level + recv[h], outside)

        steps = [functools.partial(advance, part) for part in range(PARTS)] * (bits - 1)
        return post, [begin] + steps, result, receive_rest, finish

    other_first = [lax.rem(own + half + r, heads) for r in range(heads)]
    own_first = [lax.rem(own + r, heads) for r in range(heads)]

    def spot_columns(h):
        return pl.ds(pl.multiple_of(h * DIM, DIM), DIM)

    post, stages, start_state, receive_rest, finish_forward = exchange(
        False, f_send, f_recv, f_tsend, f_trecv, f_pre,
        fs_sem, fr_sem, fts_sem, ftr_sem, fps_sem, fpr_sem,
    )

    wait(load_k)
    wait(load_v)
    for r, h in enumerate(other_first):
        row = cum_rows[pl.ds(h, 1), :]
        turned = k[:, spot_columns(h)].T.astype(F32)
        weighted_keys = (turned * jnp.exp(row[:, tokens - 1 :] - row)).astype(BF16)
        post(r, h, dot(weighted_keys, v[:, spot_columns(h)], (1, 0)))

    wait(load_q)

    def forward(h, i):
        rows = slice(i * TILE, (i + 1) * TILE)
        total_rows = None
        for j in range(i + 1):
            sources = slice(j * TILE, (j + 1) * TILE)
            scores = dot(q[rows, columns(h)], k[sources, columns(h)], (1, 1))
            spread = cum[rows, h : h + 1] - cum_rows[h : h + 1, sources]
            if i == j:
                spread = jnp.where(diagonal, spread, -1e30)
            decays = jnp.exp(spread)
            dec[h, rows, sources] = decays
            mixing = (scores * decays).astype(BF16)
            mix[h, sources, rows] = mixing.T
            part = dot(mixing, v[sources, columns(h)], (1, 0))
            total_rows = part if total_rows is None else total_rows + part
        att[rows, columns(h)] = total_rows

    def weigh_queries():
        for h in range(heads):
            turned = q[:, columns(h)].T.astype(F32)
            qt[columns(h), :] = turned.astype(BF16)
            wq[columns(h), :] = (turned * jnp.exp(cum_rows[h : h + 1, :])).astype(BF16)

    def units(work):
        return [functools.partial(work, h, i) for h in range(heads) for i in range(tiles)]

    def interleave(works, stages):
        for place, stage in enumerate(stages):
            for work in works[place] if place < len(works) else ():
                work()
            stage()

    def receive_levels():
        for copy in level_copies:
            copy.wait()

    def spread_factors():
        starting = jnp.exp(cum[...])
        ending = jnp.exp(cum[tokens - 1 : tokens, :] - cum[...])
        for h in range(heads):
            start_factor[h] = jnp.broadcast_to(starting[:, h : h + 1], (tokens, DIM))
            end_factor[h] = jnp.broadcast_to(ending[:, h : h + 1], (tokens, DIM))

    parts = units(forward)
    middle = len(parts) // 2
    interleave([[receive_levels], parts[:middle], [spread_factors] + parts[middle:]], stages)

    wait(load_gain)
    wait(load_up)
    for r, h in enumerate(own_first):
        if r == half:
            receive_rest()
        at = spot_columns(h)
        high, low = split(start_state(h))
        states[h] = jnp.concatenate([high, low], axis=1)
        queries = q[:, at]
        carried = dot(
            jnp.concatenate([queries, queries], axis=1), jnp.concatenate([high, low], axis=0), (1, 0)
        )
        value = att[:, at] + start_factor[h] * carried
        att[:, at] = value
        scaled = gain[:, at] * up[:, at].astype(F32)
        square, cross = value * value, scaled * value
        squares = square if r == 0 else squares + square
        crosses = cross if r == 0 else crosses + cross
    ones = jnp.ones((16, 2 * DIM), BF16)
    for place, addends in enumerate((squares, crosses)):
        high, low = split(addends)
        added = dot(ones, jnp.concatenate([high, low], axis=1), (1, 1))
        z_send[place : place + 1] = added[:1]
    z_copies = []
    for d in range(1, head_n):
        copy = pltpu.make_async_remote_copy(
            src_ref=z_send, dst_ref=z_recv.at[d - 1],
            send_sem=zs_sem.at[d - 1], recv_sem=zr_sem.at[d - 1],
            device_id=(me, lax.rem(zed + d, head_n)), device_id_type=MESH,
        )
        copy.start()
        z_copies.append(copy)
    weigh_queries()
    finish_forward()
    sums = z_send[...]
    for d in range(1, head_n):
        z_copies[d - 1].wait_recv()
        sums = sums + z_recv[d - 1]
    inverse = lax.rsqrt(sums[0:1] / width + EPSILON)
    factor = inverse * inverse * inverse * sums[1:2] / width
    full = jnp.concatenate([inverse, factor, jnp.zeros((DIM - 2, tokens), F32)], axis=0).T
    inverse = jnp.broadcast_to(full[:, 0:1], (tokens, DIM))
    factor = jnp.broadcast_to(full[:, 1:2], (tokens, DIM))

    post, stages, end_state, receive_rest, finish_backward = exchange(
        True, b_send, b_recv, b_tsend, b_trecv, b_pre,
        bs_sem, br_sem, bts_sem, btr_sem, bps_sem, bpr_sem,
    )
    for r, h in enumerate(other_first):
        at = spot_columns(h)
        scaled = gain[:, at] * up[:, at].astype(F32)
        value = (inverse * scaled - att[:, at] * factor).astype(BF16)
        grad[:, at] = value
        post(r, h, dot(wq[at, :], value, (1, 0)))
    for copy in z_copies:
        copy.wait_send()

    def backward(h, i):
        rows = slice(i * TILE, (i + 1) * TILE)
        grads = grad[rows, columns(h)]
        query_sum = start_factor[h, rows] * dot(
            jnp.concatenate([grads, grads], axis=1), states[h], (1, 1)
        )
        for j in range(i + 1):
            sources = slice(j * TILE, (j + 1) * TILE)
            scores = dot(grads, v[sources, columns(h)], (1, 1))
            mixing = (scores * dec[h, rows, sources]).astype(BF16)
            query_sum = query_sum + dot(mixing, k[sources, columns(h)], (1, 0))
            key_part = dot(qt[columns(h), rows], mixing, (1, 0))
            value_part = dot(mix[h, sources, rows], grads, (1, 0))
            if i == j:
                dkt[columns(h), sources] = key_part
                dvp[sources, columns(h)] = value_part
            else:
                dkt[columns(h), sources] += key_part
                dvp[sources, columns(h)] += value_part
        dq[rows, columns(h)] = query_sum.astype(BF16)
        if i == tiles - 1:
            dkp[:, columns(h)] = dkt[columns(h), :].T

    parts = units(backward)
    interleave([[], parts[:middle], parts[middle:]], stages)

    for r, h in enumerate(own_first):
        if r == half:
            receive_rest()
        at = spot_columns(h)
        high, low = split(end_state(h))
        ending = end_factor[h]
        keys, values = k[:, at], v[:, at]
        key_carried = dot(
            jnp.concatenate([values, values], axis=1), jnp.concatenate([high, low], axis=1), (1, 1)
        )
        dk[:, at] = (ending * key_carried + dkp[:, at]).astype(BF16)
        value_carried = dot(
            jnp.concatenate([keys, keys], axis=1), jnp.concatenate([high, low], axis=0), (1, 0)
        )
        dv[:, at] = (ending * value_carried + dvp[:, at]).astype(BF16)
    finish_backward()


def hand_over(*refs):
    count = (len(refs) - 1) // 2
    sem = refs[-1]
    copies = []
    for i in range(count):
        size = refs[i].shape[0] // COPIES
        for part in range(COPIES):
            rows = pl.ds(part * size, size)
            copy = pltpu.make_async_copy(
                refs[i].at[rows], refs[count + i].at[rows], sem.at[i * COPIES + part]
            )
            copy.start()
            copies.append(copy)
    for copy in copies:
        copy.wait()


def on_device(queries, keys, values, log_decay, gain, upstream):
    tokens, local = queries.shape
    heads = log_decay.shape[1]
    ctx_n, head_n = lax.axis_size("ctx"), lax.axis_size("head")
    slots = (ctx_n.bit_length() - 2) * heads * PARTS
    half = heads // 2
    wide = (tokens, local)
    message = (heads, DIM, DIM)
    chip_message = (slots, DIM // PARTS, DIM)
    states = [
        pltpu.VMEM(message, F32),
        pltpu.VMEM(message, F32),
        pltpu.VMEM(chip_message, F32),
        pltpu.VMEM(chip_message, F32),
        pltpu.VMEM((heads, DIM, DIM), F32),
    ]
    dma = pltpu.SemaphoreType.DMA
    state_sems = [
        dma((heads,)), dma((heads,)), dma((slots,)), dma((slots,)),
        dma((half * PARTS,)), dma((half * PARTS,)),
    ]
    in_vmem = pl.BlockSpec(memory_space=pltpu.VMEM)
    in_hbm = pl.BlockSpec(memory_space=pltpu.HBM)
    out = jax.ShapeDtypeStruct(wide, BF16)
    results = pl.pallas_call(
        functools.partial(kernel, ctx_n, head_n, local * head_n),
        out_shape=(pltpu.VMEM(wide, BF16),) * 3,
        in_specs=[in_hbm] * 6,
        out_specs=(in_vmem,) * 3,
        scratch_shapes=[
            pltpu.VMEM(wide, BF16),
            pltpu.VMEM(wide, BF16),
            pltpu.VMEM(wide, BF16),
            pltpu.VMEM((heads, tokens), F32),
            pltpu.VMEM((1, local), F32),
            pltpu.VMEM(wide, BF16),
            pltpu.VMEM((heads, tokens, tokens), BF16),
            pltpu.VMEM((heads, tokens, tokens), F32),
            pltpu.VMEM(wide, F32),
            pltpu.VMEM(wide, BF16),
            pltpu.VMEM((local, tokens), BF16),
            pltpu.VMEM((tokens, DIM), F32),
            pltpu.VMEM((8, tokens), F32),
            pltpu.VMEM(wide, F32),
            pltpu.VMEM(wide, F32),
            pltpu.VMEM((heads, tokens, DIM), F32),
            pltpu.VMEM((heads, tokens, DIM), F32),
            pltpu.VMEM((heads, DIM, 2 * DIM), BF16),
            pltpu.VMEM((local, tokens), BF16),
            pltpu.VMEM((local, tokens), F32),
            *states,
            *states,
            pltpu.VMEM((2, tokens), F32),
            pltpu.VMEM((head_n - 1, 2, tokens), F32),
            pltpu.VMEM((ctx_n, 8, DIM), F32),
            dma((6 * COPIES,)),
            *state_sems,
            *state_sems,
            dma((head_n - 1,)),
            dma((head_n - 1,)),
            dma((ctx_n - 1,)),
            dma((ctx_n - 1,)),
        ],
        compiler_params=pltpu.CompilerParams(
            collective_id=0, has_side_effects=True, vmem_limit_bytes=60 * 2**20
        ),
        cost_estimate=pl.CostEstimate(
            flops=16 * heads * tokens * tokens * DIM,
            bytes_accessed=14 * tokens * local,
            transcendentals=heads * tokens * tokens,
        ),
    )(queries, keys, values, log_decay.T, gain.reshape(1, -1), upstream)
    return pl.pallas_call(
        hand_over,
        out_shape=(out, out, out),
        in_specs=[in_vmem] * 3,
        out_specs=(in_hbm,) * 3,
        scratch_shapes=[dma((3 * COPIES,))],
        compiler_params=pltpu.CompilerParams(vmem_limit_bytes=8 * 2**20),
    )(*results)


def solution(mesh):
    wide = P("ctx", "head")
    return jax.shard_map(
        on_device,
        mesh=mesh,
        in_specs=(wide, wide, wide, wide, P("head"), wide),
        out_specs=(wide, wide, wide),
        check_vma=False,
    )
```

```python
import functools

import jax
import jax.numpy as jnp
from jax import lax
from jax.experimental import pallas as pl
from jax.experimental.pallas import tpu as pltpu
from jax.sharding import PartitionSpec as P

DIM = 128
TILE = 256
COPIES = 4
PARTS = 1
EPSILON = 1e-06
MESH = pl.DeviceIdType.MESH
F32 = jnp.float32
BF16 = jnp.bfloat16


def dot(a, b, dims):
    return lax.dot_general(a, b, ((dims[:1], dims[1:]), ((), ())), preferred_element_type=F32)


def split(x):
    high = x.astype(BF16)
    return high, (x - high.astype(F32)).astype(BF16)


def kernel(
    ctx_n, head_n, width,
    q_hbm, k_hbm, v_hbm, ld_hbm, gain_hbm, up_hbm,
    dq, dk, dv,
    q, k, v, ld, gain, up,
    mix, dec, att, grad, wq, cum, cum_rows, dkp, dvp, start_factor, end_factor, states, qt, dkt,
    f_send, f_recv, f_tsend, f_trecv, f_pre,
    b_send, b_recv, b_tsend, b_trecv, b_pre,
    z_send, z_recv, levels,
    in_sem,
    fs_sem, fr_sem, fts_sem, ftr_sem, fps_sem, fpr_sem,
    bs_sem, br_sem, bts_sem, btr_sem, bps_sem, bpr_sem,
    zs_sem, zr_sem, ls_sem, lr_sem,
):
    tokens = q.shape[0]
    heads = q.shape[1] // DIM
    half = heads // 2
    bits = ctx_n.bit_length() - 1
    bits_x = (bits - 1) // 2
    chips_x = 2**bits_x
    tiles = tokens // TILE
    me = lax.axis_index("ctx")
    zed = lax.axis_index("head")
    core = lax.rem(me, 2)
    own = core * half
    bit_values = [lax.rem(me // (2**b), 2) for b in range(bits)]
    partners = [me + (2**b) * (1 - 2 * bit_values[b]) for b in range(bits)]

    def load(number, src, dst, parts):
        size = src.shape[0] // parts
        copies = []
        for part in range(parts):
            rows = pl.ds(part * size, size)
            copy = pltpu.make_async_copy(
                src.at[rows], dst.at[rows], in_sem.at[number * COPIES + part]
            )
            copy.start()
            copies.append(copy)
        return copies

    def wait(copies):
        for copy in copies:
            copy.wait()

    load_ld = load(0, ld_hbm, ld, 1)
    load_k = load(1, k_hbm, k, 2)
    load_v = load(2, v_hbm, v, 2)

    barrier = pltpu.get_barrier_semaphore()
    for d in range(1, ctx_n):
        pl.semaphore_signal(
            barrier, inc=1, device_id=(lax.rem(me + d, ctx_n), zed), device_id_type=MESH
        )
    for d in range(1, head_n):
        pl.semaphore_signal(
            barrier, inc=1, device_id=(me, lax.rem(zed + d, head_n)), device_id_type=MESH
        )

    load_q = load(3, q_hbm, q, 1)
    load_gain = load(4, gain_hbm, gain, 1)
    load_up = load(5, up_hbm, up, 1)

    row_id = lax.broadcasted_iota(jnp.int32, (tokens, tokens), 0)
    col_id = lax.broadcasted_iota(jnp.int32, (tokens, tokens), 1)
    until = jnp.where(row_id <= col_id, 1.0, 0.0).astype(BF16)
    wait(load_ld)
    steps = jnp.pad(ld[...], ((0, 8 - heads), (0, 0)))
    top = steps.astype(BF16).astype(F32)
    rest = (steps - top).astype(BF16).astype(F32)
    parts = jnp.concatenate([top, rest, steps - top - rest, jnp.zeros_like(steps)], axis=0)
    sums = dot(parts.astype(BF16), until, (1, 0))
    rows_cum = sums[:8] + (sums[8:16] + sums[16:24])
    cum_rows[...] = rows_cum
    cum[...] = jnp.concatenate([rows_cum, jnp.zeros((DIM - 8, tokens), F32)], axis=0).T

    levels[me] = jnp.broadcast_to(rows_cum[:, tokens - 1 :], (8, DIM))
    pl.semaphore_wait(barrier, ctx_n + head_n - 2)
    level_copies = []
    for d in range(1, ctx_n):
        copy = pltpu.make_async_remote_copy(
            src_ref=levels.at[me], dst_ref=levels.at[me],
            send_sem=ls_sem.at[d - 1], recv_sem=lr_sem.at[d - 1],
            device_id=(lax.rem(me + d, ctx_n), zed), device_id_type=MESH,
        )
        copy.start()
        level_copies.append(copy)

    def columns(h):
        return slice(h * DIM, (h + 1) * DIM)

    diagonal = lax.broadcasted_iota(jnp.int32, (TILE, TILE), 0) >= lax.broadcasted_iota(
        jnp.int32, (TILE, TILE), 1
    )

    def exchange(rev, send, recv, tsend, trecv, pre, ss, rs, tss, trs, pss, prs):
        pending = []
        spot = ctx_n - 1 - me if rev else me
        chip = spot // 2
        row_start = chip - lax.rem(chip, chips_x)

        def remote(src, dst, s_sem, r_sem, b):
            copy = pltpu.make_async_remote_copy(
                src_ref=src, dst_ref=dst, send_sem=s_sem, recv_sem=r_sem,
                device_id=(partners[b], zed), device_id_type=MESH,
            )
            copy.start()
            pending.append(copy)
            return copy

        def span(first, last, o):
            total_level = jnp.zeros((1, DIM), F32)
            for j in range(ctx_n):
                place = (ctx_n - 1 - j if rev else j) // 2
                inside = jnp.logical_and(first <= place, place < last)
                total_level = total_level + jnp.where(inside, levels[j, pl.ds(o, 1), :], 0.0)
            return jnp.exp(total_level)

        def is_upper(b):
            return lax.rem(spot // (2**b), 2) == 1

        first = []

        def post(r, h, value):
            send[h] = value
            first.append(remote(send.at[h], recv.at[h], ss.at[r], rs.at[r], 0))

        def slot_of(b, i, second):
            head, part = i
            return (((b - 1) * half + head) * PARTS + part) * 2 + second

        copies = {}

        def publish(b, i, value, second=0):
            slot = slot_of(b, i, second)
            tsend[slot] = value
            copies[b, i, second] = remote(
                tsend.at[slot], trecv.at[slot], tss.at[slot], trs.at[slot], b
            )

        def arrived(b, i, second=0):
            copies[b, i, second].wait_recv()
            return trecv[slot_of(b, i, second)]

        def rows_of(i):
            return pl.ds(i[1] * (DIM // PARTS), DIM // PARTS)

        def finish_head(i, value):
            at = (own + i[0], rows_of(i))
            number = i[0] * PARTS + i[1]
            pre[at] = value
            copies["pre", i] = remote(pre.at[at], pre.at[at], pss.at[number], prs.at[number], 0)

        def pair(i):
            o, rows = own + i[0], rows_of(i)
            first_level = jnp.exp(levels[me, pl.ds(o, 1), :])
            other_level = jnp.exp(levels[partners[0], pl.ds(o, 1), :])
            upper = is_upper(0)
            return send[o, rows] * jnp.where(upper, 1.0, other_level) + recv[o, rows] * jnp.where(
                upper, first_level, 1.0
            )

        def straight(i):
            o = own + i[0]
            value = pair(i)
            publish(1, i, value)
            yield
            before = jnp.zeros((DIM // PARTS, DIM), F32)
            for b in range(1, bits):
                size = 2 ** (b - 1)
                upper = is_upper(b)
                group = chip - lax.rem(chip, size)
                to_chip = jnp.where(upper, span(group, chip, o), 0.0)
                upper_group = jnp.where(upper, group, group + size)
                faded = span(upper_group, upper_group + size, o)
                other = arrived(b, i)
                before = before + to_chip * other
                if b + 1 < bits:
                    value = value * jnp.where(upper, 1.0, faded) + other * jnp.where(
                        upper, faded, 1.0
                    )
                    publish(b + 1, i, value)
                    yield
            finish_head(i, before)
            yield

        def crossed(i):
            o = own + i[0]
            value = pair(i)
            column = value * span(chip + 1, row_start + chips_x, o)
            publish(bits_x + 1, i, column)
            yield
            above = jnp.zeros((DIM // PARTS, DIM), F32)
            for b in range(bits_x + 1, bits):
                size = 2 ** (b - 1)
                upper = is_upper(b)
                group = chip - lax.rem(chip, size)
                to_row = jnp.where(upper, span(group, row_start, o), 0.0)
                upper_group = jnp.where(upper, group, group + size)
                faded = span(upper_group, upper_group + size, o)
                if b + 1 == bits:
                    last_group = chip - lax.rem(chip, chips_x // 2)
                    until_end = span(row_start, last_group + chips_x // 2, o)
                other = arrived(b, i)
                above = above + to_row * other
                if b + 1 < bits:
                    column = column * jnp.where(upper, 1.0, faded) + other * jnp.where(
                        upper, faded, 1.0
                    )
                    publish(b + 1, i, column)
                    yield
            before = jnp.zeros((DIM // PARTS, DIM), F32)
            for b in range(1, bits_x + 1):
                size = 2 ** (b - 1)
                upper = is_upper(b)
                group = chip - lax.rem(chip, size)
                to_chip = jnp.where(upper, span(group, chip, o), 0.0)
                if b < bits_x:
                    publish(b, i, value)
                    publish(b, i, above, 1)
                    yield
                    other = arrived(b, i)
                    above = above + arrived(b, i, 1)
                    before = before + to_chip * other
                    upper_group = jnp.where(upper, group, group + size)
                    faded = span(upper_group, upper_group + size, o)
                    value = value * jnp.where(upper, 1.0, faded) + other * jnp.where(
                        upper, faded, 1.0
                    )
                else:
                    publish(b, i, jnp.where(upper, above, until_end * above + value))
                    yield
                    until_chip = span(row_start, chip, o)
                    before = before + until_chip * above
                    other = arrived(b, i)
                    before = before + jnp.where(upper, to_chip, until_chip) * other
            finish_head(i, before)
            yield

        routes = [
            [(crossed if i % 2 else straight)((i, part)) for i in range(half)]
            for part in range(PARTS)
        ]

        def advance(part):
            for route in routes[part]:
                next(route)

        def begin():
            for copy in first[:half]:
                copy.wait_recv()
            for part in range(PARTS):
                advance(part)

        def receive_rest():
            for copy in first[half:]:
                copy.wait_recv()
            for i in range(half):
                for part in range(PARTS):
                    copies["pre", (i, part)].wait_recv()

        def finish():
            for copy in pending:
                copy.wait_send()

        def result(h):
            outside = pre[h]
            level = jnp.exp(levels[partners[0], pl.ds(h, 1), :])
            return jnp.where(is_upper(0), outside * level + recv[h], outside)

        steps = [functools.partial(advance, part) for part in range(PARTS)] * (bits - 1)
        return post, [begin] + steps, result, receive_rest, finish

    other_first = [lax.rem(own + half + r, heads) for r in range(heads)]
    own_first = [lax.rem(own + r, heads) for r in range(heads)]

    def spot_columns(h):
        return pl.ds(pl.multiple_of(h * DIM, DIM), DIM)

    post, stages, start_state, receive_rest, finish_forward = exchange(
        False, f_send, f_recv, f_tsend, f_trecv, f_pre,
        fs_sem, fr_sem, fts_sem, ftr_sem, fps_sem, fpr_sem,
    )

    wait(load_k)
    wait(load_v)
    for r, h in enumerate(other_first):
        row = cum_rows[pl.ds(h, 1), :]
        turned = k[:, spot_columns(h)].T.astype(F32)
        weighted_keys = (turned * jnp.exp(row[:, tokens - 1 :] - row)).astype(BF16)
        post(r, h, dot(weighted_keys, v[:, spot_columns(h)], (1, 0)))

    wait(load_q)

    def forward(h, i):
        rows = slice(i * TILE, (i + 1) * TILE)
        total_rows = None
        for j in range(i + 1):
            sources = slice(j * TILE, (j + 1) * TILE)
            scores = dot(q[rows, columns(h)], k[sources, columns(h)], (1, 1))
            spread = cum[rows, h : h + 1] - cum_rows[h : h + 1, sources]
            if i == j:
                spread = jnp.where(diagonal, spread, -1e30)
            decays = jnp.exp(spread)
            dec[h, rows, sources] = decays
            mixing = (scores * decays).astype(BF16)
            mix[h, sources, rows] = mixing.T
            part = dot(mixing, v[sources, columns(h)], (1, 0))
            total_rows = part if total_rows is None else total_rows + part
        att[rows, columns(h)] = total_rows

    def weigh_queries():
        for h in range(heads):
            turned = q[:, columns(h)].T.astype(F32)
            qt[columns(h), :] = turned.astype(BF16)
            wq[columns(h), :] = (turned * jnp.exp(cum_rows[h : h + 1, :])).astype(BF16)

    def units(work):
        return [functools.partial(work, h, i) for h in range(heads) for i in range(tiles)]

    def interleave(works, stages):
        for place, stage in enumerate(stages):
            for work in works[place] if place < len(works) else ():
                work()
            stage()

    def receive_levels():
        for copy in level_copies:
            copy.wait()

    def spread_factors():
        starting = jnp.exp(cum[...])
        ending = jnp.exp(cum[tokens - 1 : tokens, :] - cum[...])
        for h in range(heads):
            start_factor[h] = jnp.broadcast_to(starting[:, h : h + 1], (tokens, DIM))
            end_factor[h] = jnp.broadcast_to(ending[:, h : h + 1], (tokens, DIM))

    parts = units(forward)
    middle = len(parts) // 2
    interleave([[receive_levels], parts[:middle], [spread_factors] + parts[middle:]], stages)

    wait(load_gain)
    wait(load_up)
    squares, crosses = [None] * tiles, [None] * tiles

    def hold_state(h):
        high, low = split(start_state(h))
        states[h] = jnp.concatenate([high, low], axis=1)

    def carry(h, i):
        at, rows = spot_columns(h), slice(i * TILE, (i + 1) * TILE)
        queries = q[rows, at]
        halves = states[h]
        carried = dot(
            jnp.concatenate([queries, queries], axis=1),
            jnp.concatenate([halves[:, :DIM], halves[:, DIM:]], axis=0),
            (1, 0),
        )
        value = att[rows, at] + start_factor[h, rows] * carried
        att[rows, at] = value
        scaled = gain[:, at] * up[rows, at].astype(F32)
        square, cross = value * value, scaled * value
        squares[i] = square if squares[i] is None else squares[i] + square
        crosses[i] = cross if crosses[i] is None else crosses[i] + cross

    z_copies = []

    def send_sums(i):
        ones = jnp.ones((16, 2 * DIM), BF16)
        for place, addends in enumerate((squares[i], crosses[i])):
            high, low = split(addends)
            added = dot(ones, jnp.concatenate([high, low], axis=1), (1, 1))
            z_send[i, place : place + 1] = added[:1]
        for d in range(1, head_n):
            number = i * (head_n - 1) + d - 1
            copy = pltpu.make_async_remote_copy(
                src_ref=z_send.at[i], dst_ref=z_recv.at[number],
                send_sem=zs_sem.at[number], recv_sem=zr_sem.at[number],
                device_id=(me, lax.rem(zed + d, head_n)), device_id_type=MESH,
            )
            copy.start()
            z_copies.append(copy)

    for h in own_first[:half]:
        hold_state(h)
        for i in range(tiles):
            carry(h, i)
    receive_rest()
    for h in own_first[half:]:
        hold_state(h)
    for i in range(tiles):
        for h in own_first[half:]:
            carry(h, i)
        send_sums(i)
    weigh_queries()
    finish_forward()
    post, stages, end_state, receive_rest, finish_backward = exchange(
        True, b_send, b_recv, b_tsend, b_trecv, b_pre,
        bs_sem, br_sem, bts_sem, btr_sem, bps_sem, bpr_sem,
    )
    state_sums = [None] * heads
    for i in range(tiles):
        rows = slice(i * TILE, (i + 1) * TILE)
        sums = z_send[i]
        for number in range(i * (head_n - 1), (i + 1) * (head_n - 1)):
            z_copies[number].wait_recv()
            sums = sums + z_recv[number]
        inverse = lax.rsqrt(sums[0:1] / width + EPSILON)
        factor = inverse * inverse * inverse * sums[1:2] / width
        full = jnp.concatenate([inverse, factor, jnp.zeros((DIM - 2, TILE), F32)], axis=0).T
        inverse = jnp.broadcast_to(full[:, 0:1], (TILE, DIM))
        factor = jnp.broadcast_to(full[:, 1:2], (TILE, DIM))
        for r, h in enumerate(other_first):
            at = spot_columns(h)
            scaled = gain[:, at] * up[rows, at].astype(F32)
            value = (inverse * scaled - att[rows, at] * factor).astype(BF16)
            grad[rows, at] = value
            added = dot(wq[at, rows], value, (1, 0))
            state_sums[r] = added if i == 0 else state_sums[r] + added
            if i == tiles - 1:
                post(r, h, state_sums[r])
    for copy in z_copies:
        copy.wait_send()

    def backward(h, i):
        rows = slice(i * TILE, (i + 1) * TILE)
        grads = grad[rows, columns(h)]
        query_sum = start_factor[h, rows] * dot(
            jnp.concatenate([grads, grads], axis=1), states[h], (1, 1)
        )
        for j in range(i + 1):
            sources = slice(j * TILE, (j + 1) * TILE)
            scores = dot(grads, v[sources, columns(h)], (1, 1))
            mixing = (scores * dec[h, rows, sources]).astype(BF16)
            query_sum = query_sum + dot(mixing, k[sources, columns(h)], (1, 0))
            key_part = dot(qt[columns(h), rows], mixing, (1, 0))
            value_part = dot(mix[h, sources, rows], grads, (1, 0))
            if i == j:
                dkt[columns(h), sources] = key_part
                dvp[sources, columns(h)] = value_part
            else:
                dkt[columns(h), sources] += key_part
                dvp[sources, columns(h)] += value_part
        dq[rows, columns(h)] = query_sum.astype(BF16)
        if i == tiles - 1:
            dkp[:, columns(h)] = dkt[columns(h), :].T

    parts = units(backward)
    interleave([[], parts[:middle], parts[middle:]], stages)

    for r, h in enumerate(own_first):
        if r == half:
            receive_rest()
        at = spot_columns(h)
        high, low = split(end_state(h))
        ending = end_factor[h]
        keys, values = k[:, at], v[:, at]
        key_carried = dot(
            jnp.concatenate([values, values], axis=1), jnp.concatenate([high, low], axis=1), (1, 1)
        )
        dk[:, at] = (ending * key_carried + dkp[:, at]).astype(BF16)
        value_carried = dot(
            jnp.concatenate([keys, keys], axis=1), jnp.concatenate([high, low], axis=0), (1, 0)
        )
        dv[:, at] = (ending * value_carried + dvp[:, at]).astype(BF16)
    finish_backward()


def hand_over(*refs):
    count = (len(refs) - 1) // 2
    sem = refs[-1]
    copies = []
    for i in range(count):
        size = refs[i].shape[0] // COPIES
        for part in range(COPIES):
            rows = pl.ds(part * size, size)
            copy = pltpu.make_async_copy(
                refs[i].at[rows], refs[count + i].at[rows], sem.at[i * COPIES + part]
            )
            copy.start()
            copies.append(copy)
    for copy in copies:
        copy.wait()


def on_device(queries, keys, values, log_decay, gain, upstream):
    tokens, local = queries.shape
    heads = log_decay.shape[1]
    ctx_n, head_n = lax.axis_size("ctx"), lax.axis_size("head")
    slots = (ctx_n.bit_length() - 2) * heads * PARTS
    half = heads // 2
    parts = tokens // TILE
    wide = (tokens, local)
    message = (heads, DIM, DIM)
    chip_message = (slots, DIM // PARTS, DIM)
    states = [
        pltpu.VMEM(message, F32),
        pltpu.VMEM(message, F32),
        pltpu.VMEM(chip_message, F32),
        pltpu.VMEM(chip_message, F32),
        pltpu.VMEM((heads, DIM, DIM), F32),
    ]
    dma = pltpu.SemaphoreType.DMA
    state_sems = [
        dma((heads,)), dma((heads,)), dma((slots,)), dma((slots,)),
        dma((half * PARTS,)), dma((half * PARTS,)),
    ]
    in_vmem = pl.BlockSpec(memory_space=pltpu.VMEM)
    in_hbm = pl.BlockSpec(memory_space=pltpu.HBM)
    out = jax.ShapeDtypeStruct(wide, BF16)
    results = pl.pallas_call(
        functools.partial(kernel, ctx_n, head_n, local * head_n),
        out_shape=(pltpu.VMEM(wide, BF16),) * 3,
        in_specs=[in_hbm] * 6,
        out_specs=(in_vmem,) * 3,
        scratch_shapes=[
            pltpu.VMEM(wide, BF16),
            pltpu.VMEM(wide, BF16),
            pltpu.VMEM(wide, BF16),
            pltpu.VMEM((heads, tokens), F32),
            pltpu.VMEM((1, local), F32),
            pltpu.VMEM(wide, BF16),
            pltpu.VMEM((heads, tokens, tokens), BF16),
            pltpu.VMEM((heads, tokens, tokens), F32),
            pltpu.VMEM(wide, F32),
            pltpu.VMEM(wide, BF16),
            pltpu.VMEM((local, tokens), BF16),
            pltpu.VMEM((tokens, DIM), F32),
            pltpu.VMEM((8, tokens), F32),
            pltpu.VMEM(wide, F32),
            pltpu.VMEM(wide, F32),
            pltpu.VMEM((heads, tokens, DIM), F32),
            pltpu.VMEM((heads, tokens, DIM), F32),
            pltpu.VMEM((heads, DIM, 2 * DIM), BF16),
            pltpu.VMEM((local, tokens), BF16),
            pltpu.VMEM((local, tokens), F32),
            *states,
            *states,
            pltpu.VMEM((parts, 2, TILE), F32),
            pltpu.VMEM((parts * (head_n - 1), 2, TILE), F32),
            pltpu.VMEM((ctx_n, 8, DIM), F32),
            dma((6 * COPIES,)),
            *state_sems,
            *state_sems,
            dma((parts * (head_n - 1),)),
            dma((parts * (head_n - 1),)),
            dma((ctx_n - 1,)),
            dma((ctx_n - 1,)),
        ],
        compiler_params=pltpu.CompilerParams(
            collective_id=0, has_side_effects=True, vmem_limit_bytes=60 * 2**20
        ),
        cost_estimate=pl.CostEstimate(
            flops=16 * heads * tokens * tokens * DIM,
            bytes_accessed=14 * tokens * local,
            transcendentals=heads * tokens * tokens,
        ),
    )(queries, keys, values, log_decay.T, gain.reshape(1, -1), upstream)
    return pl.pallas_call(
        hand_over,
        out_shape=(out, out, out),
        in_specs=[in_vmem] * 3,
        out_specs=(in_hbm,) * 3,
        scratch_shapes=[dma((3 * COPIES,))],
        compiler_params=pltpu.CompilerParams(vmem_limit_bytes=8 * 2**20),
    )(*results)


def solution(mesh):
    wide = P("ctx", "head")
    return jax.shard_map(
        on_device,
        mesh=mesh,
        in_specs=(wide, wide, wide, wide, P("head"), wide),
        out_specs=(wide, wide, wide),
        check_vma=False,
    )
```

```python
import functools

import jax
import jax.numpy as jnp
from jax import lax
from jax.experimental import pallas as pl
from jax.experimental.pallas import tpu as pltpu
from jax.sharding import PartitionSpec as P

DIM = 128
TILE = 256
COPIES = 4
PARTS = 1
EPSILON = 1e-06
MESH = pl.DeviceIdType.MESH
F32 = jnp.float32
BF16 = jnp.bfloat16


def dot(a, b, dims):
    return lax.dot_general(a, b, ((dims[:1], dims[1:]), ((), ())), preferred_element_type=F32)


def split(x):
    high = x.astype(BF16)
    return high, (x - high.astype(F32)).astype(BF16)


def kernel(
    ctx_n, head_n, width,
    q_hbm, k_hbm, v_hbm, ld_hbm, gain_hbm, up_hbm,
    dq, dk, dv,
    q, k, v, ld, gain, up,
    mix, dec, att, grad, wq, cum, cum_rows, dkp, dvp, start_factor, end_factor, states, qt, dkt,
    f_send, f_recv, f_tsend, f_trecv, f_pre,
    b_send, b_recv, b_tsend, b_trecv, b_pre,
    z_send, z_recv, levels,
    in_sem,
    fs_sem, fr_sem, fts_sem, ftr_sem, fps_sem, fpr_sem,
    bs_sem, br_sem, bts_sem, btr_sem, bps_sem, bpr_sem,
    zs_sem, zr_sem, ls_sem, lr_sem,
):
    tokens = q.shape[0]
    heads = q.shape[1] // DIM
    half = heads // 2
    bits = ctx_n.bit_length() - 1
    bits_x = (bits - 1) // 2
    chips_x = 2**bits_x
    tiles = tokens // TILE
    me = lax.axis_index("ctx")
    zed = lax.axis_index("head")
    core = lax.rem(me, 2)
    own = core * half
    bit_values = [lax.rem(me // (2**b), 2) for b in range(bits)]
    partners = [me + (2**b) * (1 - 2 * bit_values[b]) for b in range(bits)]

    def load(number, src, dst, parts):
        size = src.shape[0] // parts
        copies = []
        for part in range(parts):
            rows = pl.ds(part * size, size)
            copy = pltpu.make_async_copy(
                src.at[rows], dst.at[rows], in_sem.at[number * COPIES + part]
            )
            copy.start()
            copies.append(copy)
        return copies

    def wait(copies):
        for copy in copies:
            copy.wait()

    load_ld = load(0, ld_hbm, ld, 1)
    load_k = load(1, k_hbm, k, 2)
    load_v = load(2, v_hbm, v, 2)

    barrier = pltpu.get_barrier_semaphore()
    for d in range(1, ctx_n):
        pl.semaphore_signal(
            barrier, inc=1, device_id=(lax.rem(me + d, ctx_n), zed), device_id_type=MESH
        )
    for d in range(1, head_n):
        pl.semaphore_signal(
            barrier, inc=1, device_id=(me, lax.rem(zed + d, head_n)), device_id_type=MESH
        )

    load_q = load(3, q_hbm, q, 1)
    load_gain = load(4, gain_hbm, gain, 1)
    load_up = load(5, up_hbm, up, 1)

    row_id = lax.broadcasted_iota(jnp.int32, (tokens, tokens), 0)
    col_id = lax.broadcasted_iota(jnp.int32, (tokens, tokens), 1)
    until = jnp.where(row_id <= col_id, 1.0, 0.0).astype(BF16)
    wait(load_ld)
    steps = jnp.pad(ld[...], ((0, 8 - heads), (0, 0)))
    top = steps.astype(BF16).astype(F32)
    rest = (steps - top).astype(BF16).astype(F32)
    parts = jnp.concatenate([top, rest, steps - top - rest, jnp.zeros_like(steps)], axis=0)
    sums = dot(parts.astype(BF16), until, (1, 0))
    rows_cum = sums[:8] + (sums[8:16] + sums[16:24])
    cum_rows[...] = rows_cum
    cum[...] = jnp.concatenate([rows_cum, jnp.zeros((DIM - 8, tokens), F32)], axis=0).T

    levels[me] = jnp.broadcast_to(rows_cum[:, tokens - 1 :], (8, DIM))
    pl.semaphore_wait(barrier, ctx_n + head_n - 2)
    level_copies = []
    for d in range(1, ctx_n):
        copy = pltpu.make_async_remote_copy(
            src_ref=levels.at[me], dst_ref=levels.at[me],
            send_sem=ls_sem.at[d - 1], recv_sem=lr_sem.at[d - 1],
            device_id=(lax.rem(me + d, ctx_n), zed), device_id_type=MESH,
        )
        copy.start()
        level_copies.append(copy)

    def columns(h):
        return slice(h * DIM, (h + 1) * DIM)

    diagonal = lax.broadcasted_iota(jnp.int32, (TILE, TILE), 0) >= lax.broadcasted_iota(
        jnp.int32, (TILE, TILE), 1
    )

    def exchange(rev, send, recv, tsend, trecv, pre, ss, rs, tss, trs, pss, prs):
        pending = []
        spot = ctx_n - 1 - me if rev else me
        chip = spot // 2
        row_start = chip - lax.rem(chip, chips_x)

        def remote(src, dst, s_sem, r_sem, b):
            copy = pltpu.make_async_remote_copy(
                src_ref=src, dst_ref=dst, send_sem=s_sem, recv_sem=r_sem,
                device_id=(partners[b], zed), device_id_type=MESH,
            )
            copy.start()
            pending.append(copy)
            return copy

        def span(first, last, o):
            total_level = jnp.zeros((1, DIM), F32)
            for j in range(ctx_n):
                place = (ctx_n - 1 - j if rev else j) // 2
                inside = jnp.logical_and(first <= place, place < last)
                total_level = total_level + jnp.where(inside, levels[j, pl.ds(o, 1), :], 0.0)
            return jnp.exp(total_level)

        def is_upper(b):
            return lax.rem(spot // (2**b), 2) == 1

        first = []

        def post(r, h, value):
            send[h] = value
            first.append(remote(send.at[h], recv.at[h], ss.at[r], rs.at[r], 0))

        def slot_of(b, i, second):
            head, part = i
            return (((b - 1) * half + head) * PARTS + part) * 2 + second

        copies = {}

        def publish(b, i, value, second=0):
            slot = slot_of(b, i, second)
            tsend[slot] = value
            copies[b, i, second] = remote(
                tsend.at[slot], trecv.at[slot], tss.at[slot], trs.at[slot], b
            )

        def arrived(b, i, second=0):
            copies[b, i, second].wait_recv()
            return trecv[slot_of(b, i, second)]

        def rows_of(i):
            return pl.ds(i[1] * (DIM // PARTS), DIM // PARTS)

        def finish_head(i, value):
            at = (own + i[0], rows_of(i))
            number = i[0] * PARTS + i[1]
            pre[at] = value
            copies["pre", i] = remote(pre.at[at], pre.at[at], pss.at[number], prs.at[number], 0)

        def pair(i):
            o, rows = own + i[0], rows_of(i)
            first_level = jnp.exp(levels[me, pl.ds(o, 1), :])
            other_level = jnp.exp(levels[partners[0], pl.ds(o, 1), :])
            upper = is_upper(0)
            return send[o, rows] * jnp.where(upper, 1.0, other_level) + recv[o, rows] * jnp.where(
                upper, first_level, 1.0
            )

        def straight(i):
            o = own + i[0]
            value = pair(i)
            publish(1, i, value)
            yield
            before = jnp.zeros((DIM // PARTS, DIM), F32)
            for b in range(1, bits):
                size = 2 ** (b - 1)
                upper = is_upper(b)
                group = chip - lax.rem(chip, size)
                to_chip = jnp.where(upper, span(group, chip, o), 0.0)
                upper_group = jnp.where(upper, group, group + size)
                faded = span(upper_group, upper_group + size, o)
                other = arrived(b, i)
                before = before + to_chip * other
                if b + 1 < bits:
                    value = value * jnp.where(upper, 1.0, faded) + other * jnp.where(
                        upper, faded, 1.0
                    )
                    publish(b + 1, i, value)
                    yield
            finish_head(i, before)
            yield

        def crossed(i):
            o = own + i[0]
            value = pair(i)
            column = value * span(chip + 1, row_start + chips_x, o)
            publish(bits_x + 1, i, column)
            yield
            above = jnp.zeros((DIM // PARTS, DIM), F32)
            for b in range(bits_x + 1, bits):
                size = 2 ** (b - 1)
                upper = is_upper(b)
                group = chip - lax.rem(chip, size)
                to_row = jnp.where(upper, span(group, row_start, o), 0.0)
                upper_group = jnp.where(upper, group, group + size)
                faded = span(upper_group, upper_group + size, o)
                if b + 1 == bits:
                    last_group = chip - lax.rem(chip, chips_x // 2)
                    until_end = span(row_start, last_group + chips_x // 2, o)
                other = arrived(b, i)
                above = above + to_row * other
                if b + 1 < bits:
                    column = column * jnp.where(upper, 1.0, faded) + other * jnp.where(
                        upper, faded, 1.0
                    )
                    publish(b + 1, i, column)
                    yield
            before = jnp.zeros((DIM // PARTS, DIM), F32)
            for b in range(1, bits_x + 1):
                size = 2 ** (b - 1)
                upper = is_upper(b)
                group = chip - lax.rem(chip, size)
                to_chip = jnp.where(upper, span(group, chip, o), 0.0)
                if b < bits_x:
                    publish(b, i, value)
                    publish(b, i, above, 1)
                    yield
                    other = arrived(b, i)
                    above = above + arrived(b, i, 1)
                    before = before + to_chip * other
                    upper_group = jnp.where(upper, group, group + size)
                    faded = span(upper_group, upper_group + size, o)
                    value = value * jnp.where(upper, 1.0, faded) + other * jnp.where(
                        upper, faded, 1.0
                    )
                else:
                    publish(b, i, jnp.where(upper, above, until_end * above + value))
                    yield
                    until_chip = span(row_start, chip, o)
                    before = before + until_chip * above
                    other = arrived(b, i)
                    before = before + jnp.where(upper, to_chip, until_chip) * other
            finish_head(i, before)
            yield

        routes = [
            [(crossed if i % 2 else straight)((i, part)) for i in range(half)]
            for part in range(PARTS)
        ]

        def advance(part):
            for route in routes[part]:
                next(route)

        def begin():
            for copy in first[:half]:
                copy.wait_recv()
            for part in range(PARTS):
                advance(part)

        def receive_rest():
            for copy in first[half:]:
                copy.wait_recv()
            for i in range(half):
                for part in range(PARTS):
                    copies["pre", (i, part)].wait_recv()

        def finish():
            for copy in pending:
                copy.wait_send()

        def result(h):
            outside = pre[h]
            level = jnp.exp(levels[partners[0], pl.ds(h, 1), :])
            return jnp.where(is_upper(0), outside * level + recv[h], outside)

        steps = [functools.partial(advance, part) for part in range(PARTS)] * (bits - 1)
        return post, [begin] + steps, result, receive_rest, finish

    other_first = [lax.rem(own + half + r, heads) for r in range(heads)]
    own_first = [lax.rem(own + r, heads) for r in range(heads)]

    def spot_columns(h):
        return pl.ds(pl.multiple_of(h * DIM, DIM), DIM)

    post, stages, start_state, receive_rest, finish_forward = exchange(
        False, f_send, f_recv, f_tsend, f_trecv, f_pre,
        fs_sem, fr_sem, fts_sem, ftr_sem, fps_sem, fpr_sem,
    )

    wait(load_k)
    wait(load_v)
    for r, h in enumerate(other_first):
        row = cum_rows[pl.ds(h, 1), :]
        turned = k[:, spot_columns(h)].T.astype(F32)
        weighted_keys = (turned * jnp.exp(row[:, tokens - 1 :] - row)).astype(BF16)
        post(r, h, dot(weighted_keys, v[:, spot_columns(h)], (1, 0)))

    wait(load_q)

    def forward(h, i):
        rows = slice(i * TILE, (i + 1) * TILE)
        total_rows = None
        for j in range(i + 1):
            sources = slice(j * TILE, (j + 1) * TILE)
            scores = dot(q[rows, columns(h)], k[sources, columns(h)], (1, 1))
            spread = cum[rows, h : h + 1] - cum_rows[h : h + 1, sources]
            if i == j:
                spread = jnp.where(diagonal, spread, -1e30)
            decays = jnp.exp(spread)
            dec[h, rows, sources] = decays
            mixing = (scores * decays).astype(BF16)
            mix[h, sources, rows] = mixing.T
            part = dot(mixing, v[sources, columns(h)], (1, 0))
            total_rows = part if total_rows is None else total_rows + part
        att[rows, columns(h)] = total_rows

    def weigh_queries(chosen):
        for h in chosen:
            turned = q[:, columns(h)].T.astype(F32)
            qt[columns(h), :] = turned.astype(BF16)
            wq[columns(h), :] = (turned * jnp.exp(cum_rows[h : h + 1, :])).astype(BF16)

    def units(work):
        return [functools.partial(work, h, i) for h in range(heads) for i in range(tiles)]

    def interleave(works, stages):
        for place, stage in enumerate(stages):
            for work in works[place] if place < len(works) else ():
                work()
            stage()

    def receive_levels():
        for copy in level_copies:
            copy.wait()

    def spread_factors():
        starting = jnp.exp(cum[...])
        ending = jnp.exp(cum[tokens - 1 : tokens, :] - cum[...])
        for h in range(heads):
            start_factor[h] = jnp.broadcast_to(starting[:, h : h + 1], (tokens, DIM))
            end_factor[h] = jnp.broadcast_to(ending[:, h : h + 1], (tokens, DIM))

    parts = units(forward)
    middle = len(parts) // 2
    early = [functools.partial(weigh_queries, range(half))]
    late = [functools.partial(weigh_queries, range(half, heads)), spread_factors]
    interleave([[receive_levels], early + parts[:middle], late + parts[middle:]], stages)

    wait(load_gain)
    wait(load_up)
    for r, h in enumerate(own_first):
        if r == half:
            receive_rest()
        at = spot_columns(h)
        high, low = split(start_state(h))
        states[h] = jnp.concatenate([high, low], axis=1)
        queries = q[:, at]
        carried = dot(
            jnp.concatenate([queries, queries], axis=1), jnp.concatenate([high, low], axis=0), (1, 0)
        )
        value = att[:, at] + start_factor[h] * carried
        att[:, at] = value
        scaled = gain[:, at] * up[:, at].astype(F32)
        square, cross = value * value, scaled * value
        squares = square if r == 0 else squares + square
        crosses = cross if r == 0 else crosses + cross
    ones = jnp.ones((16, 2 * DIM), BF16)
    for place, addends in enumerate((squares, crosses)):
        high, low = split(addends)
        added = dot(ones, jnp.concatenate([high, low], axis=1), (1, 1))
        z_send[place : place + 1] = added[:1]
    z_copies = []
    for d in range(1, head_n):
        copy = pltpu.make_async_remote_copy(
            src_ref=z_send, dst_ref=z_recv.at[d - 1],
            send_sem=zs_sem.at[d - 1], recv_sem=zr_sem.at[d - 1],
            device_id=(me, lax.rem(zed + d, head_n)), device_id_type=MESH,
        )
        copy.start()
        z_copies.append(copy)
    finish_forward()
    sums = z_send[...]
    for d in range(1, head_n):
        z_copies[d - 1].wait_recv()
        sums = sums + z_recv[d - 1]
    inverse = lax.rsqrt(sums[0:1] / width + EPSILON)
    factor = inverse * inverse * inverse * sums[1:2] / width
    full = jnp.concatenate([inverse, factor, jnp.zeros((DIM - 2, tokens), F32)], axis=0).T
    inverse = jnp.broadcast_to(full[:, 0:1], (tokens, DIM))
    factor = jnp.broadcast_to(full[:, 1:2], (tokens, DIM))

    post, stages, end_state, receive_rest, finish_backward = exchange(
        True, b_send, b_recv, b_tsend, b_trecv, b_pre,
        bs_sem, br_sem, bts_sem, btr_sem, bps_sem, bpr_sem,
    )
    for r, h in enumerate(other_first):
        at = spot_columns(h)
        scaled = gain[:, at] * up[:, at].astype(F32)
        value = (inverse * scaled - att[:, at] * factor).astype(BF16)
        grad[:, at] = value
        post(r, h, dot(wq[at, :], value, (1, 0)))
    for copy in z_copies:
        copy.wait_send()

    def backward(h, i):
        rows = slice(i * TILE, (i + 1) * TILE)
        grads = grad[rows, columns(h)]
        query_sum = start_factor[h, rows] * dot(
            jnp.concatenate([grads, grads], axis=1), states[h], (1, 1)
        )
        for j in range(i + 1):
            sources = slice(j * TILE, (j + 1) * TILE)
            scores = dot(grads, v[sources, columns(h)], (1, 1))
            mixing = (scores * dec[h, rows, sources]).astype(BF16)
            query_sum = query_sum + dot(mixing, k[sources, columns(h)], (1, 0))
            key_part = dot(qt[columns(h), rows], mixing, (1, 0))
            value_part = dot(mix[h, sources, rows], grads, (1, 0))
            if i == j:
                dkt[columns(h), sources] = key_part
                dvp[sources, columns(h)] = value_part
            else:
                dkt[columns(h), sources] += key_part
                dvp[sources, columns(h)] += value_part
        dq[rows, columns(h)] = query_sum.astype(BF16)
        if i == tiles - 1:
            dkp[:, columns(h)] = dkt[columns(h), :].T

    parts = units(backward)
    interleave([[], parts[:middle], parts[middle:]], stages)

    for r, h in enumerate(own_first):
        if r == half:
            receive_rest()
        at = spot_columns(h)
        high, low = split(end_state(h))
        ending = end_factor[h]
        keys, values = k[:, at], v[:, at]
        key_carried = dot(
            jnp.concatenate([values, values], axis=1), jnp.concatenate([high, low], axis=1), (1, 1)
        )
        dk[:, at] = (ending * key_carried + dkp[:, at]).astype(BF16)
        value_carried = dot(
            jnp.concatenate([keys, keys], axis=1), jnp.concatenate([high, low], axis=0), (1, 0)
        )
        dv[:, at] = (ending * value_carried + dvp[:, at]).astype(BF16)
    finish_backward()


def hand_over(*refs):
    count = (len(refs) - 1) // 2
    sem = refs[-1]
    copies = []
    for i in range(count):
        size = refs[i].shape[0] // COPIES
        for part in range(COPIES):
            rows = pl.ds(part * size, size)
            copy = pltpu.make_async_copy(
                refs[i].at[rows], refs[count + i].at[rows], sem.at[i * COPIES + part]
            )
            copy.start()
            copies.append(copy)
    for copy in copies:
        copy.wait()


def on_device(queries, keys, values, log_decay, gain, upstream):
    tokens, local = queries.shape
    heads = log_decay.shape[1]
    ctx_n, head_n = lax.axis_size("ctx"), lax.axis_size("head")
    slots = (ctx_n.bit_length() - 2) * heads * PARTS
    half = heads // 2
    wide = (tokens, local)
    message = (heads, DIM, DIM)
    chip_message = (slots, DIM // PARTS, DIM)
    states = [
        pltpu.VMEM(message, F32),
        pltpu.VMEM(message, F32),
        pltpu.VMEM(chip_message, F32),
        pltpu.VMEM(chip_message, F32),
        pltpu.VMEM((heads, DIM, DIM), F32),
    ]
    dma = pltpu.SemaphoreType.DMA
    state_sems = [
        dma((heads,)), dma((heads,)), dma((slots,)), dma((slots,)),
        dma((half * PARTS,)), dma((half * PARTS,)),
    ]
    in_vmem = pl.BlockSpec(memory_space=pltpu.VMEM)
    in_hbm = pl.BlockSpec(memory_space=pltpu.HBM)
    out = jax.ShapeDtypeStruct(wide, BF16)
    results = pl.pallas_call(
        functools.partial(kernel, ctx_n, head_n, local * head_n),
        out_shape=(pltpu.VMEM(wide, BF16),) * 3,
        in_specs=[in_hbm] * 6,
        out_specs=(in_vmem,) * 3,
        scratch_shapes=[
            pltpu.VMEM(wide, BF16),
            pltpu.VMEM(wide, BF16),
            pltpu.VMEM(wide, BF16),
            pltpu.VMEM((heads, tokens), F32),
            pltpu.VMEM((1, local), F32),
            pltpu.VMEM(wide, BF16),
            pltpu.VMEM((heads, tokens, tokens), BF16),
            pltpu.VMEM((heads, tokens, tokens), F32),
            pltpu.VMEM(wide, F32),
            pltpu.VMEM(wide, BF16),
            pltpu.VMEM((local, tokens), BF16),
            pltpu.VMEM((tokens, DIM), F32),
            pltpu.VMEM((8, tokens), F32),
            pltpu.VMEM(wide, F32),
            pltpu.VMEM(wide, F32),
            pltpu.VMEM((heads, tokens, DIM), F32),
            pltpu.VMEM((heads, tokens, DIM), F32),
            pltpu.VMEM((heads, DIM, 2 * DIM), BF16),
            pltpu.VMEM((local, tokens), BF16),
            pltpu.VMEM((local, tokens), F32),
            *states,
            *states,
            pltpu.VMEM((2, tokens), F32),
            pltpu.VMEM((head_n - 1, 2, tokens), F32),
            pltpu.VMEM((ctx_n, 8, DIM), F32),
            dma((6 * COPIES,)),
            *state_sems,
            *state_sems,
            dma((head_n - 1,)),
            dma((head_n - 1,)),
            dma((ctx_n - 1,)),
            dma((ctx_n - 1,)),
        ],
        compiler_params=pltpu.CompilerParams(
            collective_id=0, has_side_effects=True, vmem_limit_bytes=60 * 2**20
        ),
        cost_estimate=pl.CostEstimate(
            flops=16 * heads * tokens * tokens * DIM,
            bytes_accessed=14 * tokens * local,
            transcendentals=heads * tokens * tokens,
        ),
    )(queries, keys, values, log_decay.T, gain.reshape(1, -1), upstream)
    return pl.pallas_call(
        hand_over,
        out_shape=(out, out, out),
        in_specs=[in_vmem] * 3,
        out_specs=(in_hbm,) * 3,
        scratch_shapes=[dma((3 * COPIES,))],
        compiler_params=pltpu.CompilerParams(vmem_limit_bytes=8 * 2**20),
    )(*results)


def solution(mesh):
    wide = P("ctx", "head")
    return jax.shard_map(
        on_device,
        mesh=mesh,
        in_specs=(wide, wide, wide, wide, P("head"), wide),
        out_specs=(wide, wide, wide),
        check_vma=False,
    )
```
